128 devices in a mesh: gx: 16 (over z, x), gy: 8 (over y, core).
Axes of the slice: x: 4, y: 4, z: 4, core: 2. Of those that a mesh axis runs over, the one named last changes fastest.
Arguments:
- increment: bfloat16 [64, 768, 1024], P(None, 'gx', 'gy'), may hold values from -6 to 6
- ensemble: bfloat16 [4, 64, 768, 1024], P(None, None, 'gx', 'gy'), may hold values from -6 to 6
- wind_u: bfloat16 [64, 768, 1024], P(None, 'gx', 'gy'), may hold values from -0.94921875 to 0.94921875
- wind_v: bfloat16 [64, 768, 1024], P(None, 'gx', 'gy'), may hold values from -0.94921875 to 0.94921875
- filter_length: float32 [64], replicated, may hold values from 8 to 6144
- jacobian: bfloat16 [128, 512, 64], P(('gx', 'gy')), may hold values from -0.75 to 0.75
- obs_weight: float32 [128, 512], P(('gx', 'gy')), may hold values from 0.1 to 1
- departure: bfloat16 [8192, 512, 128], P(('gx', 'gy')), may hold values from -6 to 6
- obs_home: int32 [8192], P(('gx', 'gy')), may hold values from 0 to 127, as said below
- obs_line: int32 [8192], P(('gx', 'gy')), may hold values from 0 to 47
- obs_count: int32 [8192], P(('gx', 'gy')), may hold values from 1 to 128
Outputs:
- grad_alpha: float32 [4, 64, 768, 1024], P(None, None, 'gx', 'gy')
- grad_static: float32 [64, 768, 1024], P(None, 'gx', 'gy')
The draws below stay inside these ranges and needn't reach their ends.
Inputs may be any that keep to these rules, and one draw needn't show every extreme that they name: `obs_home`: the records of one device name 64 distinct grid devices, each exactly 1 times.
All inputs are finite; a program needn't handle non-finite values.
Results may differ from the reference program's by a relative error of at most 0.003.
Values may be sent and summed in bfloat16 or wider, within the bound.
No kernel may reach another device: no remote copies, remote signals or barrier semaphores. Data moves between devices by JAX's collectives and lax.ppermute only.
A program may use at most 192 MiB of HBM per device.

```python
import math
import jax
import jax.numpy as jnp
from jax import lax

CX = 48
CY = 128
LEV = 64
CH = 512
MEM = 4
OBS_DEV = 64
HOMES = 128
MOST = 1
NX = 768
NY = 1024
RECORDS = 8192
N_GX = 16
N_GY = 8


def draw_obs_home(key, part):
    subkeys = jax.random.split(jax.random.fold_in(key, 17), 3)
    levels = jax.random.randint(subkeys[0], (HOMES,), 0, 4)
    weights = 1 + 3 * levels
    scores = jax.random.randint(subkeys[1], (HOMES, HOMES), 0, 4096) * weights[None, :]
    scores = scores * HOMES + jnp.arange(HOMES)[None, :]
    picked = lax.top_k(scores, OBS_DEV // MOST)[1]
    repeated = jnp.repeat(picked, MOST, axis=1)
    shuffle = jax.random.randint(subkeys[2], (HOMES, OBS_DEV), 0, 4096) * OBS_DEV + jnp.arange(OBS_DEV)[None, :]
    ordering = jnp.argsort(shuffle, axis=1, stable=True)
    return jnp.take_along_axis(repeated, ordering, axis=1).reshape(HOMES * OBS_DEV).astype(jnp.int32)


def touch_ends(array, stream_key, smallest, largest):
    extent = array.shape
    index_at = [jax.random.randint(jax.random.fold_in(stream_key, axis), (), 0, extent[axis]) for axis in range(len(extent))]
    array = array.at[tuple(index_at)].set(smallest)
    longest = extent.index(max(extent))
    index_at[longest] = (index_at[longest] + 1) % extent[longest]
    return array.at[tuple(index_at)].set(largest)


def shard_levels(key, shape, pieces, low, top_value):
    def one(position, shards_of):
        heights = jax.random.uniform(jax.random.fold_in(jax.random.fold_in(key, 6), position), (shards_of,), jnp.float32, low / len(pieces), top_value / len(pieces))
        return jnp.repeat(jnp.exp(heights), shape[position] // shards_of).reshape((-1,) + (1,) * (len(shape) - position - 1))

    level = one(*pieces[0])
    for cut in pieces[1:]:
        level = level * one(*cut)
    return level


def bell_draw(rng, shape, scale, bound, shards=(), held_as=jnp.bfloat16):
    drawn = scale * jax.random.normal(rng, shape, jnp.float32)
    if shards:
        drawn = drawn * shard_levels(rng, shape, shards, -0.22, 0.18)
    return jnp.clip(drawn, -bound, bound).astype(held_as)


def setup_inputs(seed: int = 0) -> dict:
    key_of = jax.random.split(jax.random.key(seed), 12)
    increment = bell_draw(key_of[0], (LEV, NX, NY), 1.0, 6.0, ((1, 16), (2, 8)))
    ensemble = bell_draw(key_of[1], (MEM, LEV, NX, NY), 1.0, 6.0, ((2, 16), (3, 8)))
    wind_u = jnp.clip(jax.random.uniform(key_of[2], (LEV, NX, NY), jnp.float32, -0.94921875, 0.94921875) * shard_levels(key_of[2], (LEV, NX, NY), ((1, 16), (2, 8)), -0.4, 0.0), -0.94921875, 0.94921875).astype(jnp.bfloat16)
    wind_v = jnp.clip(jax.random.uniform(key_of[3], (LEV, NX, NY), jnp.float32, -0.94921875, 0.94921875) * shard_levels(key_of[3], (LEV, NX, NY), ((1, 16), (2, 8)), -0.4, 0.0), -0.94921875, 0.94921875).astype(jnp.bfloat16)
    filter_length = jnp.clip(jnp.exp(jax.random.uniform(key_of[4], (LEV,), jnp.float32, math.log(8.0), math.log(6144.0))), 8.0, 6144.0)
    jacobian = bell_draw(key_of[5], (HOMES, CH, LEV), LEV ** -0.5, 0.75, ((0, 128),))
    obs_weight = jnp.clip(jnp.exp(math.log(1.0) - 2.3025851 * jax.random.uniform(key_of[6], (HOMES, CH), jnp.float32) ** shard_levels(key_of[6], (HOMES, CH), ((0, 128),), -0.2, 0.2)), 0.1, 1.0)
    departure = bell_draw(key_of[7], (RECORDS, CH, CY), 1.0, 6.0, ((0, 128),))
    obs_home = draw_obs_home(jax.random.fold_in(key_of[11], 71), 0)
    obs_line = touch_ends(jax.random.randint(key_of[9], (RECORDS,), 0, CX), jax.random.fold_in(key_of[9], 1), 0, CX - 1).astype(jnp.int32)
    obs_count = touch_ends(jax.random.randint(key_of[10], (RECORDS,), 1, CY + 1), jax.random.fold_in(key_of[10], 1), 1, CY).astype(jnp.int32)
    return dict(increment=increment, ensemble=ensemble, wind_u=wind_u, wind_v=wind_v, filter_length=filter_length, jacobian=jacobian, obs_weight=obs_weight, departure=departure, obs_home=obs_home, obs_line=obs_line, obs_count=obs_count)


def recursive(field, coefs, decays, backward):

    def advance(state, column):
        updated = coefs[:, None] * column + decays[:, None] * state
        return (updated, updated)
    start = jnp.zeros(field.shape[1:], jnp.float32)
    _, result = lax.scan(advance, start, field, reverse=backward)
    return result

def smooth(field, forward_coef, backward_coef, decays):
    turned = jnp.transpose(field, (1, 0, 2))
    turned = recursive(turned, forward_coef, decays, False)
    turned = recursive(turned, backward_coef, decays, True)
    turned = jnp.transpose(turned, (2, 1, 0))
    turned = recursive(turned, forward_coef, decays, False)
    turned = recursive(turned, backward_coef, decays, True)
    return jnp.transpose(turned, (1, 2, 0))

def transport_x(static, speed):
    padded = jnp.pad(static, ((0, 0), (1, 1), (0, 0)))
    return static + jnp.maximum(speed, 0.0) * (padded[:, :-2, :] - static) + jnp.maximum(-speed, 0.0) * (padded[:, 2:, :] - static)

def transport_y(static, speed):
    padded = jnp.pad(static, ((0, 0), (0, 0), (1, 1)))
    return static + jnp.maximum(speed, 0.0) * (padded[:, :, :-2] - static) + jnp.maximum(-speed, 0.0) * (padded[:, :, 2:] - static)

def one_home(packed):
    matrix, weight_row, gathered, observed_dep, counts = packed
    matrix = matrix.astype(jnp.float32)
    predicted = jnp.einsum('cl,oly->ocy', matrix, gathered.astype(jnp.float32))
    observed = (jnp.arange(CY, dtype=jnp.int32)[None, :] < counts[:, None]).astype(jnp.float32)
    weighted = (weight_row[None, :, None] * (predicted - observed_dep.astype(jnp.float32)) * observed[:, None, :]).astype(jnp.bfloat16)
    adjoint = jnp.einsum('cl,ocy->oly', matrix, weighted.astype(jnp.float32))
    return adjoint.astype(jnp.bfloat16)

def reference(increment, ensemble, wind_u, wind_v, filter_length, jacobian, obs_weight, departure, obs_home, obs_line, obs_count):
    home_count = N_GX * N_GY
    grid_x = obs_home // N_GY * CX + obs_line
    grid_y = obs_home % N_GY
    block_id = (grid_x * N_GY + grid_y).astype(jnp.int32)
    blocks = jnp.transpose(increment.reshape(LEV, NX, N_GY, CY), (1, 2, 0, 3)).reshape(NX * N_GY, LEV, CY)
    gathered = blocks[block_id].reshape(home_count, OBS_DEV, LEV, CY)
    adjoints = lax.map(one_home, (jacobian, obs_weight, gathered, departure.reshape(home_count, OBS_DEV, CH, CY), obs_count.reshape(home_count, OBS_DEV)))
    summed = jnp.zeros((NX * N_GY, LEV, CY), jnp.float32).at[block_id].add(adjoints.reshape(home_count * OBS_DEV, LEV, CY).astype(jnp.float32))
    grad_obs = jnp.transpose(summed.reshape(NX, N_GY, LEV, CY), (2, 0, 1, 3)).reshape(LEV, NX, NY)
    decays = jnp.exp(-1.0 / filter_length)
    forward_coef = jnp.sqrt(-jnp.expm1(-2.0 / filter_length))
    backward_coef = -jnp.expm1(-1.0 / filter_length)
    grad_alpha = lax.map(lambda member: smooth(member.astype(jnp.float32) * grad_obs, forward_coef, backward_coef, decays), ensemble)
    static = smooth(grad_obs, forward_coef, backward_coef, decays)
    speed_x = wind_u.astype(jnp.float32)
    speed_y = wind_v.astype(jnp.float32)
    for sweep_index in range(3):
        static = transport_x(static, speed_x)
        static = transport_y(static, speed_y)
    return (grad_alpha, static)
```

```python
import functools

import jax
import jax.numpy as jnp
import numpy as np
from jax import lax
from jax.experimental import pallas as pl
from jax.experimental.pallas import tpu as pltpu
from jax.sharding import PartitionSpec as P

GX, GY = "gx", "gy"
BOTH = (GX, GY)
CHUNKS = 1
MIB = 2**20
F32, BF16 = jnp.float32, jnp.bfloat16

NT = (((1,), (1,)), ((), ()))
TN = (((0,), (0,)), ((), ()))


def vmem():
    return pl.BlockSpec(memory_space=pltpu.VMEM)


def smem():
    return pl.BlockSpec(memory_space=pltpu.SMEM)


def params(mib):
    return pltpu.CompilerParams(vmem_limit_bytes=mib * MIB)


def split(value):
    high = value.astype(BF16)
    return high, (value - high.astype(F32)).astype(BF16)


def sensor_kernel(jt_ref, w_ref, meta_ref, b_ref, out_ref):
    lev = jt_ref.shape[0]
    high, low = split(jt_ref[...].astype(F32) * w_ref[...])
    b_ref[:lev] = high
    b_ref[lev:] = low
    a = lax.dot_general(high, jt_ref[...], NT, preferred_element_type=F32)
    a += lax.dot_general(low, jt_ref[...], NT, preferred_element_type=F32)
    row = lax.broadcasted_iota(jnp.int32, a.shape, 0)
    col = lax.broadcasted_iota(jnp.int32, a.shape, 1)
    high = a.astype(BF16).astype(F32)
    packed = jnp.where(col >= row, high, a - high)
    diagonal = jnp.sum(jnp.where(col == row, a - high, 0.0), axis=0, keepdims=True)
    half = lev // 2
    out_ref[:half] = jnp.concatenate([packed[:half], packed[half:]], axis=1).astype(BF16)
    meta = meta_ref[...].astype(F32)
    first = lax.broadcasted_iota(jnp.int32, meta.shape, 0) == 0
    out_ref[half:] = jnp.where(
        first, jnp.concatenate([diagonal, jnp.zeros_like(diagonal)], axis=1), meta
    ).astype(BF16)


def records_kernel(home_ref, count_ref, b_ref, dep_ref, *outs):
    step, per = pl.program_id(0), dep_ref.shape[0]
    lev = b_ref.shape[0] // 2
    part = lev // len(outs)

    @pl.when(step == 0)
    def _():
        for out in outs:
            out[...] = jnp.zeros_like(out)

    lane = lax.broadcasted_iota(jnp.int32, (lev, dep_ref.shape[2]), 1)
    for k in range(per):
        both = jnp.dot(b_ref[...], dep_ref[k], preferred_element_type=F32)
        q = both[:lev] + both[lev:]
        q = jnp.where(lane < count_ref[step * per + k], q, 0.0).astype(BF16)
        for c, out in enumerate(outs):
            out[home_ref[step * per + k]] = q[c * part : (c + 1) * part]


def columns_kernel(line_ref, count_ref, gathered_ref, inc_ref, g_ref, x_ref):
    lev, nx, ny = inc_ref.shape
    for l in range(lev):
        x_ref[pl.ds(l * nx, nx), :] = inc_ref[l].astype(F32)
    g_ref[...] = jnp.zeros_like(g_ref)
    lane = lax.broadcasted_iota(jnp.int32, (lev, ny), 1)
    half = lev // 2
    eye = lax.broadcasted_iota(jnp.int32, (lev, lev), 0) == lax.broadcasted_iota(
        jnp.int32, (lev, lev), 1
    )
    group = 4

    def some(i, carry):
        found = []
        for k in range(group):
            s = i * group + k
            at = jnp.maximum(line_ref[s] - 1, 0)
            x = x_ref[pl.ds(at, lev, stride=nx), :].astype(BF16)
            kept = gathered_ref[s, :half].astype(F32)
            m = jnp.concatenate([kept[:, :lev], kept[:, lev:]], axis=0)
            diagonal = gathered_ref[s, half : half + 16].astype(F32)[:1, :lev]
            other = jnp.where(eye, diagonal, jnp.transpose(m))
            y = jnp.dot(
                jnp.concatenate([m, other], axis=1).astype(BF16),
                jnp.concatenate([x, x], axis=0),
                preferred_element_type=F32,
            )
            found.append((at, jnp.where(lane < count_ref[s], y, 0.0)))
        for at, y in found:
            g_ref[pl.ds(at, lev, stride=nx), :] += y
        return carry

    lax.fori_loop(0, line_ref.shape[0] // group, some, 0)


def lay_fields(g1_ref, g2_ref, ens_ref, f_ref):
    members, block, nx, ny = ens_ref.shape
    rows = (members + 1) * nx + 8
    for l in range(block):
        g = g1_ref[l] - g2_ref[l]
        f_ref[pl.ds(l * rows + members * nx, nx), :] = g
        for m in range(members):
            f_ref[pl.ds(l * rows + m * nx, nx), :] = ens_ref[m, l].astype(F32) * g


def edges_kernel(g1_ref, g2_ref, ens_ref, coef_ref, h_ref, f_ref, tmp_ref):
    members, block, nx, ny = ens_ref.shape
    fields = members + 1
    rows = fields * nx + 8
    lay_fields(g1_ref, g2_ref, ens_ref, f_ref)

    for base in range(0, block, 8):
        d, fc, rt, d49, inv = (coef_ref[k, base : base + 8] for k in range(5))

        def line(m, x, base=base):
            return f_ref[pl.ds(base * rows + m * nx + x, 8, stride=rows), :]

        ahead = [line(m, 0) for m in range(fields)]
        back = [line(m, nx - 1) for m in range(fields)]
        for x in range(1, nx):
            for m in range(fields):
                ahead[m] = d * ahead[m] + line(m, x)
                back[m] = d * back[m] + line(m, nx - 1 - x)

        def put(row, value, base=base):
            tmp_ref[pl.ds(base * 16 + row, 8, stride=16), :] = value

        for m in range(fields):
            put(3 + m, fc * ahead[m])
            put(8 + m, rt * (back[m] - d49 * ahead[m]))
        e, p = ahead[members], back[members]
        f0, f1 = line(members, 0), line(members, 1)
        f46, f47 = line(members, nx - 2), line(members, nx - 1)
        d48, d47 = d49 * inv, d49 * inv * inv
        p1 = (p - f0) * inv
        p2 = (p1 - f1) * inv
        put(0, rt * (p - d49 * e))
        put(1, rt * (d * f0 + p1 - d48 * e))
        put(2, rt * (d * (d * f0 + f1) + p2 - d47 * e))
        e1 = (e - f47) * inv
        e2 = (e1 - f46) * inv
        put(13, rt * (e2 + d * (f46 + d * f47) - d * d * d * d * e))
        put(14, rt * (e1 + d * f47 - d * d * d * e))
        put(15, rt * (e - d * d * e))
    for l in range(block):
        h_ref[l] = tmp_ref[pl.ds(l * 16, 16), :]


def scan_x_kernel(in_ref, coef_ref, out_ref):
    count, levels = in_ref.shape[:2]
    row = lax.broadcasted_iota(jnp.int32, (8, in_ref.shape[3]), 0)
    for l in range(levels):
        d0, d1, kappa, a0, b0, a1, b1 = (coef_ref[k, l] for k in range(7))
        first, second = [], []
        for g in range(count):
            v = in_ref[g, l].astype(F32)
            first.append(v[:8])
            second.append(v[8:])
        ahead = [jnp.zeros_like(row, F32)]
        for g in range(count - 1):
            ahead.append(first[g] + d0 * ahead[g])
        turned = [pltpu.roll(a, 5, 0) for a in ahead]
        back = [jnp.zeros_like(row, F32)] * count
        for g in range(count - 1, 0, -1):
            back[g - 1] = second[g] + kappa * turned[g] + d1 * back[g]
        static = [(ahead[g][7:8], back[g][4:5]) for g in range(count)]
        low = [first[g] + a0 * static[g][0] + b0 * static[g][1] for g in range(count)]
        high = [second[g] + a1 * static[g][0] + b1 * static[g][1] for g in range(count)]
        none = jnp.zeros_like(row, F32)
        for g in range(count):
            after = low[g + 1] if g + 1 < count else none
            before = high[g - 1] if g > 0 else none
            out_ref[g, l] = jnp.concatenate(
                [jnp.where(row < 3, after, ahead[g]), jnp.where(row < 5, back[g], before)], axis=0
            )


def filter_x_kernel(
    g1_ref,
    g2_ref,
    ens_ref,
    fb_ref,
    coef_ref,
    v_ref,
    hi_ref,
    lo_ref,
    es_ref,
    right_ref,
    left_ref,
    f_ref,
    xs_ref,
    st_ref,
    ey_ref,
):
    members, block, nx, _ = ens_ref.shape
    fields = members + 1
    used = fields * nx
    rows = used + 8
    lay_fields(g1_ref, g2_ref, ens_ref, f_ref)
    deep = hi_ref.shape[1]
    wide = deep + 8
    for l in range(block):
        st_ref[pl.ds(l * 16, 16), :] = fb_ref[l]
    for base in range(0, block, 8):
        d, fc, bc = (coef_ref[k, base : base + 8] for k in range(3))

        def at(m, x, base=base):
            return pl.ds(base * wide + m * nx + x, 8, stride=wide)

        state = [st_ref[pl.ds(base * 16 + 3 + m, 8, stride=16), :] for m in range(fields)]
        for x in range(nx):
            for m in range(fields):
                f = f_ref[pl.ds(base * rows + m * nx + x, 8, stride=rows), :]
                state[m] = fc * f + d * state[m]
                xs_ref[at(m, x), :] = state[m]
        state = [st_ref[pl.ds(base * 16 + 8 + m, 8, stride=16), :] for m in range(fields)]
        for x in range(nx - 1, -1, -1):
            for m in range(fields):
                state[m] = bc * xs_ref[at(m, x), :] + d * state[m]
                xs_ref[at(m, x), :] = state[m]
    row = lax.broadcasted_iota(jnp.int32, (8, f_ref.shape[1]), 0)
    for l in range(block):
        after, before = st_ref[pl.ds(l * 16, 8), :], st_ref[pl.ds(l * 16 + 8, 8), :]
        halo = jnp.where(row < 3, after, jnp.where(row < 5, 0.0, before))
        xs_ref[pl.ds(l * wide + used, 8), :] = halo
        xs_ref[pl.ds(l * wide + used + 8, 8), :] = jnp.zeros_like(halo)
        hi, lo = split(xs_ref[pl.ds(l * wide, deep), :])
        hi_ref[l] = hi
        lo_ref[l] = lo
        one = lax.dot_general(v_ref[l], hi, NT, preferred_element_type=F32)
        two = lax.dot_general(v_ref[l], lo, NT, preferred_element_type=F32)
        ey_ref[pl.ds(l, 8, stride=block), :] = (one[:8] + one[8:] + two[:8])[:, : deep // 2]
        ey_ref[pl.ds(8 * block + l, 8, stride=block), :] = (one[:8] + one[8:] + two[:8])[
            :, deep // 2 :
        ]

    def both(q, side):
        return ey_ref[pl.ds((8 * side + q) * block, block), :].astype(BF16)

    for q in range(2):
        for side in range(2):
            got = both(q, side)
            lanes = pl.ds(side * got.shape[1], got.shape[1])
            for k in range(es_ref.shape[0]):
                es_ref[k, q, :, lanes] = got
    for q in range(3):
        left_ref[q] = both(1 + q, 1)
        right_ref[q] = both(4 + q, 1)


def scan_y_kernel(me_ref, es_ref, fl_ref, fr_ref, coef_ref, out_ref, ahead_ref, back_ref, tmp_ref):
    count, _, lev, lanes = es_ref.shape
    half = lanes // 2
    me = me_ref[0]
    decay, kappa = coef_ref[0], coef_ref[1]
    for side in range(2):
        part = pl.ds(side * half, half)
        state = jnp.zeros((lev, half), F32)
        ahead_ref[0, :, part] = state
        for k in range(count - 1):
            state = es_ref[k, 0, :, part].astype(F32) + decay * state
            ahead_ref[k + 1, :, part] = state
        state = jnp.zeros((lev, half), F32)
        back_ref[count - 1, :, part] = state
        for k in range(count - 1, 0, -1):
            state = (
                es_ref[k, 1, :, part].astype(F32)
                + kappa * ahead_ref[k, :, part]
                + decay * state
            )
            back_ref[k - 1, :, part] = state
    none = jnp.zeros((lev, half), F32)

    def put(q, side, value):
        tmp_ref[side, pl.ds(q, lev, stride=16), :] = value

    for side in range(2):
        part = pl.ds(side * half, half)
        for first, ref in ((0, ahead_ref), (3, back_ref)):
            value = ref[me, :, part]
            high = value.astype(BF16).astype(F32)
            put(first, side, high)
            put(first + 1, side, value - high)
            put(first + 2, side, high)
        for q in (6, 7, 14, 15):
            put(q, side, none)
    before, after = jnp.maximum(me - 1, 0), jnp.minimum(me + 1, count - 1)
    part = pl.ds(half, half)
    for q in range(3):
        put(8 + q, 0, none)
        put(11 + q, 0, none)
        value = (
            fl_ref[q].astype(F32)
            + coef_ref[2 + q] * ahead_ref[before, :, part]
            + coef_ref[5 + q] * back_ref[before, :, part]
        )
        put(8 + q, 1, jnp.where(me > 0, value, 0.0))
        value = (
            fr_ref[q].astype(F32)
            + coef_ref[8 + q] * ahead_ref[after, :, part]
            + coef_ref[11 + q] * back_ref[after, :, part]
        )
        put(11 + q, 1, jnp.where(me < count - 1, value, 0.0))
    for side in range(2):
        out_ref[:, pl.ds(side * half, half)] = tmp_ref[side].astype(BF16)


def final_kernel(hi_ref, lo_ref, nh_ref, nl_ref, fb_ref, ab_ref, u_ref, v_ref, *rest):
    alpha_ref, static_ref = rest[-2:]
    block = hi_ref.shape[0]
    members, _, nx, ny = alpha_ref.shape
    first = members * nx
    deep = nx + 8
    wide = 2 * ny
    for l in range(block):
        hi = hi_ref[l]
        more = lax.dot_general(
            fb_ref[pl.ds(l * 16, 16), :], ab_ref[l], TN, preferred_element_type=F32
        )
        got = jnp.dot(hi, nh_ref[l], preferred_element_type=F32)
        got += jnp.dot(hi, nl_ref[l], preferred_element_type=F32)
        got += jnp.dot(lo_ref[l], nh_ref[l], preferred_element_type=F32)
        got += more[:, :ny]
        for m in range(members):
            alpha_ref[m, l] = got[m * nx : (m + 1) * nx]
        s = jnp.concatenate(
            [got[first : first + deep], more[first : first + deep, ny:]], axis=1
        )
        u, v = u_ref[l].astype(F32), v_ref[l].astype(F32)
        up, vp = u > 0.0, v > 0.0
        u, v = jnp.abs(u), jnp.abs(v)
        for _ in range(3):
            s = s + u * (jnp.where(up, pltpu.roll(s, 1, 0), pltpu.roll(s, deep - 1, 0)) - s)
            s = s + v * (jnp.where(vp, pltpu.roll(s, 1, 1), pltpu.roll(s, wide - 1, 1)) - s)
        static_ref[l] = s[:nx, :ny]


def sent_to_all(array, axis):
    copies = jnp.broadcast_to(array[None], (lax.axis_size(axis), *array.shape))
    return lax.all_to_all(copies, axis, split_axis=0, concat_axis=0, tiled=True)


def from_before(array, axis):
    count = lax.axis_size(axis)
    return lax.ppermute(array, axis, [(i, i + 1) for i in range(count - 1)])


def from_after(array, axis):
    count = lax.axis_size(axis)
    return lax.ppermute(array, axis, [(i + 1, i) for i in range(count - 1)])


def wind_rows_kernel(u_ref, v_ref, first_ref, last_ref):
    nx = u_ref.shape[1]
    for l in range(u_ref.shape[0]):
        u, v = u_ref[l].astype(F32), v_ref[l].astype(F32)
        first_ref[l] = jnp.concatenate([u[:8], v[:8]], axis=0).astype(BF16)
        last_ref[l] = jnp.concatenate([u[nx - 8 :], v[nx - 8 :]], axis=0).astype(BF16)


def taller(u_ref, v_ref, before_ref, after_ref, l):
    before, after = before_ref[l].astype(F32), after_ref[l].astype(F32)
    row = lax.broadcasted_iota(jnp.int32, (8, before.shape[1]), 0)
    both = []
    for k, ref in enumerate((u_ref, v_ref)):
        part = slice(8 * k, 8 * k + 8)
        halo = jnp.where(row < 3, after[part], jnp.where(row > 4, before[part], 0.0))
        both.append(jnp.concatenate([ref[l].astype(F32), halo], axis=0))
    return both


def wind_columns_kernel(u_ref, v_ref, before_ref, after_ref, pick_ref, right_ref, left_ref):
    for l in range(u_ref.shape[0]):
        u, v = taller(u_ref, v_ref, before_ref, after_ref, l)
        gap = jnp.zeros((8, u.shape[1]), F32)
        both = jnp.concatenate([u, gap, v, gap], axis=0).astype(BF16)
        got = lax.dot_general(pick_ref[...], both, NT, preferred_element_type=F32)
        half = got.shape[1] // 2
        for k, ref in enumerate((right_ref, left_ref)):
            some = got[8 * k : 8 * k + 8]
            ref[l] = jnp.concatenate([some[:, :half], some[:, half:]], axis=0).astype(BF16)


def wind_pad_kernel(
    u_ref, v_ref, before_ref, after_ref, left_ref, right_ref, place_ref, out_u_ref, out_v_ref
):
    ny = u_ref.shape[2]
    for l in range(u_ref.shape[0]):
        u, v = taller(u_ref, v_ref, before_ref, after_ref, l)
        sides = jnp.concatenate([left_ref[l], right_ref[l]], axis=0)
        got = lax.dot_general(sides, place_ref[...], TN, preferred_element_type=F32)[: len(u)]
        out_u_ref[l] = jnp.concatenate([u, got[:, :ny]], axis=1).astype(BF16)
        out_v_ref[l] = jnp.concatenate([v, got[:, ny:]], axis=1).astype(BF16)


def levels(*shape):
    return pl.BlockSpec((16, *shape), lambda i: (i, *(0 for _ in shape)))


def whole(*shape):
    return pl.BlockSpec(shape, lambda i: tuple(0 for _ in shape))


def wind_halos(wind_u, wind_v):
    lev, nx, ny = wind_u.shape
    deep = nx + 16
    steps = (lev // 16,)
    first, last = pl.pallas_call(
        wind_rows_kernel,
        grid=steps,
        in_specs=[levels(nx, ny)] * 2,
        out_specs=(levels(16, ny),) * 2,
        out_shape=(jax.ShapeDtypeStruct((lev, 16, ny), BF16),) * 2,
        name="wind_rows",
    )(wind_u, wind_v)
    before, after = from_before(last, GX), from_after(first, GX)
    pick = np.zeros((16, ny), np.float32)
    for k in range(3):
        pick[k, ny - 3 + k] = pick[8 + k, k] = 1
    right, left = pl.pallas_call(
        wind_columns_kernel,
        grid=steps,
        in_specs=[levels(nx, ny)] * 2 + [levels(16, ny)] * 2 + [whole(16, ny)],
        out_specs=(levels(16, deep),) * 2,
        out_shape=(jax.ShapeDtypeStruct((lev, 16, deep), BF16),) * 2,
        name="wind_columns",
    )(wind_u, wind_v, before, after, jnp.asarray(pick, BF16))
    return before, after, from_before(right, GY), from_after(left, GY)


def padded_winds(wind_u, wind_v, halos):
    lev, nx, ny = wind_u.shape
    deep = nx + 16
    place = np.zeros((32, 2 * ny), np.float32)
    for k in range(3):
        place[k, ny - 3 + k] = place[16 + k, k] = 1
        place[8 + k, 2 * ny - 3 + k] = place[24 + k, ny + k] = 1
    return pl.pallas_call(
        wind_pad_kernel,
        grid=(lev // 16,),
        in_specs=[levels(nx, ny)] * 2
        + [levels(16, ny)] * 2
        + [levels(16, deep)] * 2
        + [whole(32, 2 * ny)],
        out_specs=(levels(nx + 8, 2 * ny),) * 2,
        out_shape=(jax.ShapeDtypeStruct((lev, nx + 8, 2 * ny), BF16),) * 2,
        name="wind_pad",
    )(wind_u, wind_v, *halos, jnp.asarray(place, BF16))


def product(length, count, i, j):
    ratio = -jnp.expm1(-1.0 / length) / jnp.sqrt(-jnp.expm1(-2.0 / length))
    last = jnp.maximum(i, j)
    return ratio * jnp.exp(-jnp.abs(i - j) / length) * -jnp.expm1(-2.0 * (count - last) / length)


def entered(length, count, i):
    ratio = jnp.expm1(-1.0 / length) / jnp.expm1(-2.0 / length)
    return ratio * jnp.exp(-(i + 1.0) / length) * -jnp.expm1(-2.0 * (count - i) / length)


def body(
    increment,
    ensemble,
    wind_u,
    wind_v,
    filter_length,
    jacobian,
    obs_weight,
    departure,
    obs_home,
    obs_line,
    obs_count,
):
    count_x, count_y = lax.axis_size(GX), lax.axis_size(GY)
    homes = count_x * count_y
    pos_x, pos_y = lax.axis_index(GX), lax.axis_index(GY)
    lev, nx, ny = increment.shape
    members = ensemble.shape[0]
    channels = jacobian.shape[1]
    records = obs_home.shape[0]
    part = lev // CHUNKS
    share = part // count_x
    rows = (members + 1) * nx + 8
    deep = rows + 8

    named = (obs_home[:, None] == jnp.arange(homes, dtype=jnp.int32)[None, :]).astype(jnp.int32)
    table = jnp.stack(
        [
            jnp.sum(named * (obs_line[:, None] + 1), axis=0),
            jnp.sum(named * obs_count[:, None], axis=0),
        ]
    ).astype(BF16)
    meta = jnp.pad(table, ((1, 13), (0, 128 - homes)))
    jt = jnp.transpose(jacobian[0])
    b, mine = pl.pallas_call(
        sensor_kernel,
        out_shape=(
            jax.ShapeDtypeStruct((2 * lev, channels), BF16),
            jax.ShapeDtypeStruct((lev // 2 + 16, 2 * lev), BF16),
        ),
        in_specs=[vmem()] * 3,
        out_specs=(vmem(), vmem()),
        name="sensor",
    )(jt, obs_weight, meta)
    gathered = sent_to_all(mine, BOTH)

    per = min(8, records)
    qs = pl.pallas_call(
        records_kernel,
        grid_spec=pltpu.PrefetchScalarGridSpec(
            num_scalar_prefetch=2,
            grid=(records // per,),
            in_specs=[
                pl.BlockSpec((2 * lev, channels), lambda i, *_: (0, 0)),
                pl.BlockSpec((per, channels, ny), lambda i, *_: (i, 0, 0)),
            ],
            out_specs=[pl.BlockSpec((homes, part, ny), lambda i, *_: (0, 0, 0))] * CHUNKS,
        ),
        out_shape=[jax.ShapeDtypeStruct((homes, part, ny), BF16)] * CHUNKS,
        compiler_params=params(56),
        name="records",
    )(obs_home, obs_count, b, departure)
    qs, wind_u, wind_v = lax.optimization_barrier((qs, wind_u, wind_v))
    winds = wind_halos(wind_u, wind_v)
    qs, winds = lax.optimization_barrier((qs, winds))
    arrived = [lax.all_to_all(q, BOTH, split_axis=0, concat_axis=0, tiled=True) for q in qs]

    seen = lax.dynamic_slice_in_dim(
        gathered[:, lev // 2 + 1 : lev // 2 + 3, :], pos_x * count_y + pos_y, 1, axis=2
    )[:, :, 0].astype(jnp.int32)
    asked, counts = seen[:, 0], seen[:, 1]
    g1 = pl.pallas_call(
        columns_kernel,
        out_shape=jax.ShapeDtypeStruct((lev * nx, ny), F32),
        in_specs=[smem(), smem(), vmem(), vmem()],
        out_specs=vmem(),
        scratch_shapes=[pltpu.VMEM((lev * nx, ny), F32)],
        compiler_params=params(24),
        cost_estimate=pl.CostEstimate(flops=2**33, bytes_accessed=2**23, transcendentals=0),
        name="columns",
    )(asked, counts, gathered, increment).reshape(lev, nx, ny)
    select = (asked[:, None] == jnp.arange(1, nx + 1, dtype=jnp.int32)[None, :]).astype(BF16)

    length = filter_length
    fc = jnp.sqrt(-jnp.expm1(-2.0 / length))
    bc = -jnp.expm1(-1.0 / length)
    d = jnp.exp(-1.0 / length)

    def wide(columns, tail):
        got = jnp.stack(columns).reshape(len(columns), lev, *(1 for _ in tail))
        return jnp.broadcast_to(got, (len(columns), lev, *tail))

    coef_e = wide([d, fc, bc / fc, jnp.exp(-(nx + 1.0) / length), jnp.exp(1.0 / length)], (ny,))
    coef_f = wide([d, fc, bc], (ny,))
    jump, zero = jnp.exp(-nx / length), jnp.zeros_like(length)
    low = [entered(length, nx, float(i)) for i in range(3)]
    high = [entered(length, nx, float(nx - 3 + i)) for i in range(3)]
    low_b = [jnp.exp(-(nx - i) / length) for i in range(3)]
    high_b = [jnp.exp(-(3.0 - i) / length) for i in range(3)]
    kappa = entered(length, nx, 0.0)
    table_x = jnp.stack(
        [
            jnp.stack(line)
            for line in (
                [zero] * 3 + [jump] * 5,
                [jump] * 5 + [zero] * 3,
                [kappa] * 5 + [zero] * 3,
                low + [zero] * 5,
                low_b + [zero] * 5,
                [zero] * 5 + high,
                [zero] * 5 + high_b,
            )
        ]
    )
    table_x = jnp.transpose(table_x, (0, 2, 1))
    cells = jnp.arange(ny, dtype=F32)
    big = product(length[:, None, None], ny, cells[None, :, None], cells[None, None, :])
    nh, nl = split(big)
    edge = jnp.stack(
        [fc[:, None] * jnp.exp(-(ny - 1.0 - cells)[None] / length[:, None])]
        + [
            product(length[:, None], ny, float(i), cells[None, :])
            for i in (0, 1, 2, ny - 3, ny - 2, ny - 1)
        ]
        + [jnp.zeros((lev, ny), F32)],
        axis=1,
    )
    edge = jnp.concatenate(split(edge), axis=1)
    enter_a = entered(length[:, None], ny, cells[None, :])
    enter_b = jnp.exp(-(ny - cells)[None, :] / length[:, None])
    ah, al = split(enter_a)
    bh, bl = split(enter_b)
    none = jnp.zeros((lev, ny), BF16)
    place = jnp.stack([jnp.arange(ny) == k for k in (ny - 3, ny - 2, ny - 1, 0, 1, 2)]).astype(BF16)
    blank = jnp.zeros((8, ny), BF16)
    place = jnp.concatenate([blank, place, blank[:2]], axis=0)
    spread = jnp.concatenate(
        [
            jnp.stack([ah, ah, al, bh, bh, bl] + [none] * 10, axis=1),
            jnp.broadcast_to(place[None], (lev, 16, ny)),
        ],
        axis=2,
    )
    coef_y = wide(
        [jnp.exp(-ny / length), entered(length, ny, 0.0)]
        + [entered(length, ny, ny - 3.0 + i) for i in range(3)]
        + [jnp.exp(-(3.0 - i) / length) for i in range(3)]
        + [entered(length, ny, float(i)) for i in range(3)]
        + [jnp.exp(-(ny - float(i)) / length) for i in range(3)],
        (ny,),
    )
    halo_u, halo_v = padded_winds(wind_u, wind_v, winds)
    arrived, halo_u, halo_v, g1 = lax.optimization_barrier((arrived, halo_u, halo_v, g1))

    alpha = static = None
    for c in range(CHUNKS):
        g2 = jnp.einsum("sx,sly->lxy", select, arrived[c], preferred_element_type=F32)
        steps = part // 16
        off = c * steps
        h = pl.pallas_call(
            edges_kernel,
            grid=(steps,),
            in_specs=[
                pl.BlockSpec((16, nx, ny), lambda i, off=off: (off + i, 0, 0)),
                pl.BlockSpec((16, nx, ny), lambda i: (i, 0, 0)),
                pl.BlockSpec((members, 16, nx, ny), lambda i, off=off: (0, off + i, 0, 0)),
                pl.BlockSpec((5, 16, ny), lambda i, off=off: (0, off + i, 0)),
            ],
            out_specs=pl.BlockSpec((16, 16, ny), lambda i: (i, 0, 0)),
            out_shape=jax.ShapeDtypeStruct((part, 16, ny), F32),
            scratch_shapes=[pltpu.VMEM((16 * rows, ny), F32), pltpu.VMEM((16 * 16, ny), F32)],
            compiler_params=params(56),
            name=f"edges_{c}",
        )(g1, g2, ensemble, coef_e)
        h = lax.all_to_all(
            h.reshape(count_x, share, 16, ny), GX, split_axis=0, concat_axis=0, tiled=True
        )
        mine_x = lax.dynamic_slice_in_dim(table_x, c * part + pos_x * share, share, axis=1)
        mine_x = jnp.broadcast_to(mine_x[:, :, :, None], (7, share, 8, ny))
        h = pl.pallas_call(
            scan_x_kernel,
            out_shape=jax.ShapeDtypeStruct(h.shape, F32),
            in_specs=[vmem(), vmem()],
            out_specs=vmem(),
            name=f"scan_x_{c}",
        )(h, mine_x)
        h = lax.all_to_all(h, GX, split_axis=0, concat_axis=0, tiled=True).reshape(part, 16, ny)
        hi, lo, es, to_right, to_left = pl.pallas_call(
            filter_x_kernel,
            grid=(steps,),
            in_specs=[
                pl.BlockSpec((16, nx, ny), lambda i, off=off: (off + i, 0, 0)),
                pl.BlockSpec((16, nx, ny), lambda i: (i, 0, 0)),
                pl.BlockSpec((members, 16, nx, ny), lambda i, off=off: (0, off + i, 0, 0)),
                pl.BlockSpec((16, 16, ny), lambda i: (i, 0, 0)),
                pl.BlockSpec((3, 16, ny), lambda i, off=off: (0, off + i, 0)),
                pl.BlockSpec((16, 16, ny), lambda i, off=off: (off + i, 0, 0)),
            ],
            out_specs=(
                pl.BlockSpec((16, deep, ny), lambda i: (i, 0, 0)),
                pl.BlockSpec((16, deep, ny), lambda i: (i, 0, 0)),
                pl.BlockSpec((count_y, 2, 16, deep), lambda i: (0, 0, i, 0)),
                pl.BlockSpec((3, 16, ny), lambda i: (0, i, 0)),
                pl.BlockSpec((3, 16, ny), lambda i: (0, i, 0)),
            ),
            out_shape=(
                jax.ShapeDtypeStruct((part, deep, ny), BF16),
                jax.ShapeDtypeStruct((part, deep, ny), BF16),
                jax.ShapeDtypeStruct((count_y, 2, part, deep), BF16),
                jax.ShapeDtypeStruct((3, part, ny), BF16),
                jax.ShapeDtypeStruct((3, part, ny), BF16),
            ),
            scratch_shapes=[
                pltpu.VMEM((16 * rows, ny), F32),
                pltpu.VMEM((16 * (deep + 8), ny), F32),
                pltpu.VMEM((16 * 16, ny), F32),
                pltpu.VMEM((16 * 16, ny), F32),
            ],
            compiler_params=params(56),
            name=f"filter_x_{c}",
        )(g1, g2, ensemble, h, coef_f, edge)
        es = lax.all_to_all(es, GY, split_axis=0, concat_axis=0, tiled=True)
        from_left = from_before(to_right, GY)
        from_right = from_after(to_left, GY)
        fb = pl.pallas_call(
            scan_y_kernel,
            out_shape=jax.ShapeDtypeStruct((part * 16, deep), BF16),
            in_specs=[smem()] + [vmem()] * 4,
            out_specs=vmem(),
            scratch_shapes=[
                pltpu.VMEM((count_y, part, deep), F32),
                pltpu.VMEM((count_y, part, deep), F32),
                pltpu.VMEM((2, part * 16, deep // 2), F32),
            ],
            compiler_params=params(16),
            name=f"scan_y_{c}",
        )(pos_y.reshape(1), es, from_left, from_right, coef_y[:, c * part : (c + 1) * part])
        steps = part // 8
        off = c * steps
        extra = () if c == 0 else (alpha, static)
        alpha, static = pl.pallas_call(
            final_kernel,
            grid=(steps,),
            in_specs=[
                pl.BlockSpec((8, deep, ny), lambda i: (i, 0, 0)),
                pl.BlockSpec((8, deep, ny), lambda i: (i, 0, 0)),
                pl.BlockSpec((8, ny, ny), lambda i, off=off: (off + i, 0, 0)),
                pl.BlockSpec((8, ny, ny), lambda i, off=off: (off + i, 0, 0)),
                pl.BlockSpec((8 * 16, deep), lambda i: (i, 0)),
                pl.BlockSpec((8, 16, 2 * ny), lambda i, off=off: (off + i, 0, 0)),
                pl.BlockSpec((8, nx + 8, 2 * ny), lambda i, off=off: (off + i, 0, 0)),
                pl.BlockSpec((8, nx + 8, 2 * ny), lambda i, off=off: (off + i, 0, 0)),
            ]
            + [pl.BlockSpec(memory_space=pl.ANY)] * len(extra),
            out_specs=(
                pl.BlockSpec((members, 8, nx, ny), lambda i, off=off: (0, off + i, 0, 0)),
                pl.BlockSpec((8, nx, ny), lambda i, off=off: (off + i, 0, 0)),
            ),
            out_shape=(
                jax.ShapeDtypeStruct((members, lev, nx, ny), F32),
                jax.ShapeDtypeStruct((lev, nx, ny), F32),
            ),
            input_output_aliases={8: 0, 9: 1} if extra else {},
            compiler_params=params(56),
            name=f"final_{c}",
        )(hi, lo, nh, nl, fb, spread, halo_u, halo_v, *extra)
    return alpha, static


def solution(mesh):
    grid = P(None, GX, GY)
    placed = (
        grid,
        P(None, None, GX, GY),
        grid,
        grid,
        P(),
        P(BOTH, None, None),
        P(BOTH, None),
        P(BOTH, None, None),
        P(BOTH),
        P(BOTH),
        P(BOTH),
    )
    return jax.shard_map(
        body,
        mesh=mesh,
        in_specs=placed,
        out_specs=(P(None, None, GX, GY), grid),
        check_vma=False,
    )
```

```python
import functools

import jax
import jax.numpy as jnp
import numpy as np
from jax import lax
from jax.experimental import pallas as pl
from jax.experimental.pallas import tpu as pltpu
from jax.sharding import PartitionSpec as P

GX, GY = "gx", "gy"
BOTH = (GX, GY)
CHUNKS = 1
MIB = 2**20
F32, BF16 = jnp.float32, jnp.bfloat16

NT = (((1,), (1,)), ((), ()))
TN = (((0,), (0,)), ((), ()))


def vmem():
    return pl.BlockSpec(memory_space=pltpu.VMEM)


def smem():
    return pl.BlockSpec(memory_space=pltpu.SMEM)


def params(mib):
    return pltpu.CompilerParams(vmem_limit_bytes=mib * MIB)


def split(value):
    high = value.astype(BF16)
    return high, (value - high.astype(F32)).astype(BF16)


def sensor_kernel(jt_ref, w_ref, meta_ref, b_ref, out_ref):
    lev = jt_ref.shape[0]
    high, low = split(jt_ref[...].astype(F32) * w_ref[...])
    b_ref[:lev] = high
    b_ref[lev:] = low
    a = lax.dot_general(high, jt_ref[...], NT, preferred_element_type=F32)
    a += lax.dot_general(low, jt_ref[...], NT, preferred_element_type=F32)
    row = lax.broadcasted_iota(jnp.int32, a.shape, 0)
    col = lax.broadcasted_iota(jnp.int32, a.shape, 1)
    high = a.astype(BF16).astype(F32)
    packed = jnp.where(col >= row, high, a - high)
    diagonal = jnp.sum(jnp.where(col == row, a - high, 0.0), axis=0, keepdims=True)
    half = lev // 2
    packed = jnp.concatenate([packed[:half], packed[half:]], axis=1)
    meta = meta_ref[...].astype(F32)
    first = lax.broadcasted_iota(jnp.int32, meta.shape, 0) == 0
    meta = jnp.where(first, jnp.concatenate([diagonal, jnp.zeros_like(diagonal)], axis=1), meta)
    whole = jnp.concatenate([packed, meta], axis=0).astype(BF16)

    def copy(k, carry):
        out_ref[k] = whole
        return carry

    lax.fori_loop(0, out_ref.shape[0], copy, 0, unroll=8)


def records_kernel(home_ref, count_ref, b_ref, dep_ref, *outs):
    step, per = pl.program_id(0), dep_ref.shape[0]
    lev = b_ref.shape[0] // 2
    part = lev // len(outs)

    @pl.when(step == 0)
    def _():
        for out in outs:
            out[...] = jnp.zeros_like(out)

    lane = lax.broadcasted_iota(jnp.int32, (lev, dep_ref.shape[2]), 1)
    for k in range(per):
        both = jnp.dot(b_ref[...], dep_ref[k], preferred_element_type=F32)
        q = both[:lev] + both[lev:]
        q = jnp.where(lane < count_ref[step * per + k], q, 0.0).astype(BF16)
        for c, out in enumerate(outs):
            out[home_ref[step * per + k]] = q[c * part : (c + 1) * part]


def columns_kernel(line_ref, count_ref, gathered_ref, inc_ref, g_ref, x_ref):
    lev, nx, ny = inc_ref.shape
    for l in range(lev):
        x_ref[pl.ds(l * nx, nx), :] = inc_ref[l].astype(F32)
    g_ref[...] = jnp.zeros_like(g_ref)
    lane = lax.broadcasted_iota(jnp.int32, (lev, ny), 1)
    half = lev // 2
    eye = lax.broadcasted_iota(jnp.int32, (lev, lev), 0) == lax.broadcasted_iota(
        jnp.int32, (lev, lev), 1
    )
    group = 4

    def some(i, carry):
        found = []
        for k in range(group):
            s = i * group + k
            at = jnp.maximum(line_ref[s] - 1, 0)
            x = x_ref[pl.ds(at, lev, stride=nx), :].astype(BF16)
            kept = gathered_ref[s, :half].astype(F32)
            m = jnp.concatenate([kept[:, :lev], kept[:, lev:]], axis=0)
            diagonal = gathered_ref[s, half : half + 16].astype(F32)[:1, :lev]
            other = jnp.where(eye, diagonal, jnp.transpose(m))
            y = jnp.dot(
                jnp.concatenate([m, other], axis=1).astype(BF16),
                jnp.concatenate([x, x], axis=0),
                preferred_element_type=F32,
            )
            found.append((at, jnp.where(lane < count_ref[s], y, 0.0)))
        for at, y in found:
            g_ref[pl.ds(at, lev, stride=nx), :] += y
        return carry

    lax.fori_loop(0, line_ref.shape[0] // group, some, 0)


def lay_fields(g1_ref, g2_ref, ens_ref, f_ref):
    members, block, nx, ny = ens_ref.shape
    rows = (members + 1) * nx + 8
    for l in range(block):
        g = g1_ref[l] - g2_ref[l]
        f_ref[pl.ds(l * rows + members * nx, nx), :] = g
        for m in range(members):
            f_ref[pl.ds(l * rows + m * nx, nx), :] = ens_ref[m, l].astype(F32) * g


def edges_kernel(g1_ref, g2_ref, ens_ref, coef_ref, h_ref, f_ref, tmp_ref):
    members, block, nx, ny = ens_ref.shape
    fields = members + 1
    rows = fields * nx + 8
    lay_fields(g1_ref, g2_ref, ens_ref, f_ref)

    for base in range(0, block, 8):
        d, fc, rt, d49, inv = (coef_ref[k, base : base + 8] for k in range(5))

        def line(m, x, base=base):
            return f_ref[pl.ds(base * rows + m * nx + x, 8, stride=rows), :]

        ahead = [line(m, 0) for m in range(fields)]
        back = [line(m, nx - 1) for m in range(fields)]
        for x in range(1, nx):
            for m in range(fields):
                ahead[m] = d * ahead[m] + line(m, x)
                back[m] = d * back[m] + line(m, nx - 1 - x)

        def put(row, value, base=base):
            tmp_ref[pl.ds(base * 16 + row, 8, stride=16), :] = value

        for m in range(fields):
            put(3 + m, fc * ahead[m])
            put(8 + m, rt * (back[m] - d49 * ahead[m]))
        e, p = ahead[members], back[members]
        f0, f1 = line(members, 0), line(members, 1)
        f46, f47 = line(members, nx - 2), line(members, nx - 1)
        d48, d47 = d49 * inv, d49 * inv * inv
        p1 = (p - f0) * inv
        p2 = (p1 - f1) * inv
        put(0, rt * (p - d49 * e))
        put(1, rt * (d * f0 + p1 - d48 * e))
        put(2, rt * (d * (d * f0 + f1) + p2 - d47 * e))
        e1 = (e - f47) * inv
        e2 = (e1 - f46) * inv
        put(13, rt * (e2 + d * (f46 + d * f47) - d * d * d * d * e))
        put(14, rt * (e1 + d * f47 - d * d * d * e))
        put(15, rt * (e - d * d * e))
    for l in range(block):
        h_ref[l] = tmp_ref[pl.ds(l * 16, 16), :]


def scan_x_kernel(in_ref, coef_ref, out_ref):
    count, levels = in_ref.shape[:2]
    row = lax.broadcasted_iota(jnp.int32, (8, in_ref.shape[3]), 0)
    for l in range(levels):
        d0, d1, kappa, a0, b0, a1, b1 = (coef_ref[k, l] for k in range(7))
        first, second = [], []
        for g in range(count):
            v = in_ref[g, l].astype(F32)
            first.append(v[:8])
            second.append(v[8:])
        ahead = [jnp.zeros_like(row, F32)]
        for g in range(count - 1):
            ahead.append(first[g] + d0 * ahead[g])
        turned = [pltpu.roll(a, 5, 0) for a in ahead]
        back = [jnp.zeros_like(row, F32)] * count
        for g in range(count - 1, 0, -1):
            back[g - 1] = second[g] + kappa * turned[g] + d1 * back[g]
        static = [(ahead[g][7:8], back[g][4:5]) for g in range(count)]
        low = [first[g] + a0 * static[g][0] + b0 * static[g][1] for g in range(count)]
        high = [second[g] + a1 * static[g][0] + b1 * static[g][1] for g in range(count)]
        none = jnp.zeros_like(row, F32)
        for g in range(count):
            after = low[g + 1] if g + 1 < count else none
            before = high[g - 1] if g > 0 else none
            out_ref[g, l] = jnp.concatenate(
                [jnp.where(row < 3, after, ahead[g]), jnp.where(row < 5, back[g], before)], axis=0
            )


def filter_x_kernel(
    g1_ref,
    g2_ref,
    ens_ref,
    fb_ref,
    coef_ref,
    v_ref,
    hi_ref,
    lo_ref,
    es_ref,
    right_ref,
    left_ref,
    f_ref,
    xs_ref,
    st_ref,
    ey_ref,
):
    members, block, nx, _ = ens_ref.shape
    fields = members + 1
    used = fields * nx
    rows = used + 8
    lay_fields(g1_ref, g2_ref, ens_ref, f_ref)
    deep = hi_ref.shape[1]
    wide = deep + 8
    for l in range(block):
        st_ref[pl.ds(l * 16, 16), :] = fb_ref[l]
    for base in range(0, block, 8):
        d, fc, bc = (coef_ref[k, base : base + 8] for k in range(3))

        def at(m, x, base=base):
            return pl.ds(base * wide + m * nx + x, 8, stride=wide)

        state = [st_ref[pl.ds(base * 16 + 3 + m, 8, stride=16), :] for m in range(fields)]
        for x in range(nx):
            for m in range(fields):
                f = f_ref[pl.ds(base * rows + m * nx + x, 8, stride=rows), :]
                state[m] = fc * f + d * state[m]
                xs_ref[at(m, x), :] = state[m]
        state = [st_ref[pl.ds(base * 16 + 8 + m, 8, stride=16), :] for m in range(fields)]
        for x in range(nx - 1, -1, -1):
            for m in range(fields):
                state[m] = bc * xs_ref[at(m, x), :] + d * state[m]
                xs_ref[at(m, x), :] = state[m]
    row = lax.broadcasted_iota(jnp.int32, (8, f_ref.shape[1]), 0)
    for l in range(block):
        after, before = st_ref[pl.ds(l * 16, 8), :], st_ref[pl.ds(l * 16 + 8, 8), :]
        halo = jnp.where(row < 3, after, jnp.where(row < 5, 0.0, before))
        xs_ref[pl.ds(l * wide + used, 8), :] = halo
        xs_ref[pl.ds(l * wide + used + 8, 8), :] = jnp.zeros_like(halo)
        hi, lo = split(xs_ref[pl.ds(l * wide, deep), :])
        hi_ref[l] = hi
        lo_ref[l] = lo
        one = lax.dot_general(v_ref[l], hi, NT, preferred_element_type=F32)
        two = lax.dot_general(v_ref[l], lo, NT, preferred_element_type=F32)
        ey_ref[pl.ds(l, 8, stride=block), :] = (one[:8] + one[8:] + two[:8])[:, : deep // 2]
        ey_ref[pl.ds(8 * block + l, 8, stride=block), :] = (one[:8] + one[8:] + two[:8])[
            :, deep // 2 :
        ]

    def both(q, side):
        return ey_ref[pl.ds((8 * side + q) * block, block), :].astype(BF16)

    for q in range(2):
        for side in range(2):
            got = both(q, side)
            lanes = pl.ds(side * got.shape[1], got.shape[1])
            for k in range(es_ref.shape[0]):
                es_ref[k, q, :, lanes] = got
    for q in range(3):
        left_ref[q] = both(1 + q, 1)
        right_ref[q] = both(4 + q, 1)


def scan_y_kernel(me_ref, es_ref, fl_ref, fr_ref, coef_ref, out_ref, ahead_ref, back_ref, tmp_ref):
    count, _, lev, lanes = es_ref.shape
    half = lanes // 2
    me = me_ref[0]
    decay, kappa = coef_ref[0], coef_ref[1]
    for side in range(2):
        part = pl.ds(side * half, half)
        state = jnp.zeros((lev, half), F32)
        ahead_ref[0, :, part] = state
        for k in range(count - 1):
            state = es_ref[k, 0, :, part].astype(F32) + decay * state
            ahead_ref[k + 1, :, part] = state
        state = jnp.zeros((lev, half), F32)
        back_ref[count - 1, :, part] = state
        for k in range(count - 1, 0, -1):
            state = (
                es_ref[k, 1, :, part].astype(F32)
                + kappa * ahead_ref[k, :, part]
                + decay * state
            )
            back_ref[k - 1, :, part] = state
    none = jnp.zeros((lev, half), F32)

    def put(q, side, value):
        tmp_ref[side, pl.ds(q, lev, stride=16), :] = value

    for side in range(2):
        part = pl.ds(side * half, half)
        for first, ref in ((0, ahead_ref), (3, back_ref)):
            value = ref[me, :, part]
            high = value.astype(BF16).astype(F32)
            put(first, side, high)
            put(first + 1, side, value - high)
            put(first + 2, side, high)
        for q in (6, 7, 14, 15):
            put(q, side, none)
    before, after = jnp.maximum(me - 1, 0), jnp.minimum(me + 1, count - 1)
    part = pl.ds(half, half)
    for q in range(3):
        put(8 + q, 0, none)
        put(11 + q, 0, none)
        value = (
            fl_ref[q].astype(F32)
            + coef_ref[2 + q] * ahead_ref[before, :, part]
            + coef_ref[5 + q] * back_ref[before, :, part]
        )
        put(8 + q, 1, jnp.where(me > 0, value, 0.0))
        value = (
            fr_ref[q].astype(F32)
            + coef_ref[8 + q] * ahead_ref[after, :, part]
            + coef_ref[11 + q] * back_ref[after, :, part]
        )
        put(11 + q, 1, jnp.where(me < count - 1, value, 0.0))
    for side in range(2):
        out_ref[:, pl.ds(side * half, half)] = tmp_ref[side].astype(BF16)


def final_kernel(hi_ref, lo_ref, nh_ref, nl_ref, fb_ref, ab_ref, u_ref, v_ref, *rest):
    alpha_ref, static_ref = rest[-2:]
    block = hi_ref.shape[0]
    members, _, nx, ny = alpha_ref.shape
    first = members * nx
    deep = nx + 8
    wide = 2 * ny
    for l in range(block):
        hi = hi_ref[l]
        more = lax.dot_general(
            fb_ref[pl.ds(l * 16, 16), :], ab_ref[l], TN, preferred_element_type=F32
        )
        got = jnp.dot(hi, nh_ref[l], preferred_element_type=F32)
        got += jnp.dot(hi, nl_ref[l], preferred_element_type=F32)
        got += jnp.dot(lo_ref[l], nh_ref[l], preferred_element_type=F32)
        got += more[:, :ny]
        for m in range(members):
            alpha_ref[m, l] = got[m * nx : (m + 1) * nx]
        s = jnp.concatenate(
            [got[first : first + deep], more[first : first + deep, ny:]], axis=1
        )
        u, v = u_ref[l].astype(F32), v_ref[l].astype(F32)
        up, vp = u > 0.0, v > 0.0
        u, v = jnp.abs(u), jnp.abs(v)
        for _ in range(3):
            s = s + u * (jnp.where(up, pltpu.roll(s, 1, 0), pltpu.roll(s, deep - 1, 0)) - s)
            s = s + v * (jnp.where(vp, pltpu.roll(s, 1, 1), pltpu.roll(s, wide - 1, 1)) - s)
        static_ref[l] = s[:nx, :ny]


def from_before(array, axis):
    count = lax.axis_size(axis)
    return lax.ppermute(array, axis, [(i, i + 1) for i in range(count - 1)])


def from_after(array, axis):
    count = lax.axis_size(axis)
    return lax.ppermute(array, axis, [(i + 1, i) for i in range(count - 1)])


def wind_rows_kernel(u_ref, v_ref, first_ref, last_ref):
    nx = u_ref.shape[1]
    for l in range(u_ref.shape[0]):
        u, v = u_ref[l].astype(F32), v_ref[l].astype(F32)
        first_ref[l] = jnp.concatenate([u[:8], v[:8]], axis=0).astype(BF16)
        last_ref[l] = jnp.concatenate([u[nx - 8 :], v[nx - 8 :]], axis=0).astype(BF16)


def taller(u_ref, v_ref, before_ref, after_ref, l):
    before, after = before_ref[l].astype(F32), after_ref[l].astype(F32)
    row = lax.broadcasted_iota(jnp.int32, (8, before.shape[1]), 0)
    both = []
    for k, ref in enumerate((u_ref, v_ref)):
        part = slice(8 * k, 8 * k + 8)
        halo = jnp.where(row < 3, after[part], jnp.where(row > 4, before[part], 0.0))
        both.append(jnp.concatenate([ref[l].astype(F32), halo], axis=0))
    return both


def wind_columns_kernel(u_ref, v_ref, before_ref, after_ref, pick_ref, right_ref, left_ref):
    for l in range(u_ref.shape[0]):
        u, v = taller(u_ref, v_ref, before_ref, after_ref, l)
        gap = jnp.zeros((8, u.shape[1]), F32)
        both = jnp.concatenate([u, gap, v, gap], axis=0).astype(BF16)
        got = lax.dot_general(pick_ref[...], both, NT, preferred_element_type=F32)
        half = got.shape[1] // 2
        for k, ref in enumerate((right_ref, left_ref)):
            some = got[8 * k : 8 * k + 8]
            ref[l] = jnp.concatenate([some[:, :half], some[:, half:]], axis=0).astype(BF16)


def wind_pad_kernel(
    u_ref, v_ref, before_ref, after_ref, left_ref, right_ref, place_ref, out_u_ref, out_v_ref
):
    ny = u_ref.shape[2]
    for l in range(u_ref.shape[0]):
        u, v = taller(u_ref, v_ref, before_ref, after_ref, l)
        sides = jnp.concatenate([left_ref[l], right_ref[l]], axis=0)
        got = lax.dot_general(sides, place_ref[...], TN, preferred_element_type=F32)[: len(u)]
        out_u_ref[l] = jnp.concatenate([u, got[:, :ny]], axis=1).astype(BF16)
        out_v_ref[l] = jnp.concatenate([v, got[:, ny:]], axis=1).astype(BF16)


def levels(*shape):
    return pl.BlockSpec((16, *shape), lambda i: (i, *(0 for _ in shape)))


def whole(*shape):
    return pl.BlockSpec(shape, lambda i: tuple(0 for _ in shape))


def wind_ends(wind_u, wind_v):
    lev, nx, ny = wind_u.shape
    steps = (lev // 16,)
    first, last = pl.pallas_call(
        wind_rows_kernel,
        grid=steps,
        in_specs=[levels(nx, ny)] * 2,
        out_specs=(levels(16, ny),) * 2,
        out_shape=(jax.ShapeDtypeStruct((lev, 16, ny), BF16),) * 2,
        compiler_params=params(8),
        name="wind_rows",
    )(wind_u, wind_v)
    return from_before(last, GX), from_after(first, GX)


def wind_sides(wind_u, wind_v, before, after):
    lev, nx, ny = wind_u.shape
    deep = nx + 16
    steps = (lev // 16,)
    pick = np.zeros((16, ny), np.float32)
    for k in range(3):
        pick[k, ny - 3 + k] = pick[8 + k, k] = 1
    right, left = pl.pallas_call(
        wind_columns_kernel,
        grid=steps,
        in_specs=[levels(nx, ny)] * 2 + [levels(16, ny)] * 2 + [whole(16, ny)],
        out_specs=(levels(16, deep),) * 2,
        out_shape=(jax.ShapeDtypeStruct((lev, 16, deep), BF16),) * 2,
        compiler_params=params(8),
        name="wind_columns",
    )(wind_u, wind_v, before, after, jnp.asarray(pick, BF16))
    return from_before(right, GY), from_after(left, GY)


def padded_winds(wind_u, wind_v, halos):
    lev, nx, ny = wind_u.shape
    deep = nx + 16
    place = np.zeros((32, 2 * ny), np.float32)
    for k in range(3):
        place[k, ny - 3 + k] = place[16 + k, k] = 1
        place[8 + k, 2 * ny - 3 + k] = place[24 + k, ny + k] = 1
    return pl.pallas_call(
        wind_pad_kernel,
        grid=(lev // 16,),
        in_specs=[levels(nx, ny)] * 2
        + [levels(16, ny)] * 2
        + [levels(16, deep)] * 2
        + [whole(32, 2 * ny)],
        out_specs=(levels(nx + 8, 2 * ny),) * 2,
        out_shape=(jax.ShapeDtypeStruct((lev, nx + 8, 2 * ny), BF16),) * 2,
        compiler_params=params(8),
        name="wind_pad",
    )(wind_u, wind_v, *halos, jnp.asarray(place, BF16))


def product(length, count, i, j):
    ratio = -jnp.expm1(-1.0 / length) / jnp.sqrt(-jnp.expm1(-2.0 / length))
    last = jnp.maximum(i, j)
    return ratio * jnp.exp(-jnp.abs(i - j) / length) * -jnp.expm1(-2.0 * (count - last) / length)


def entered(length, count, i):
    ratio = jnp.expm1(-1.0 / length) / jnp.expm1(-2.0 / length)
    return ratio * jnp.exp(-(i + 1.0) / length) * -jnp.expm1(-2.0 * (count - i) / length)


def body(
    increment,
    ensemble,
    wind_u,
    wind_v,
    filter_length,
    jacobian,
    obs_weight,
    departure,
    obs_home,
    obs_line,
    obs_count,
):
    count_x, count_y = lax.axis_size(GX), lax.axis_size(GY)
    homes = count_x * count_y
    pos_x, pos_y = lax.axis_index(GX), lax.axis_index(GY)
    lev, nx, ny = increment.shape
    members = ensemble.shape[0]
    channels = jacobian.shape[1]
    records = obs_home.shape[0]
    part = lev // CHUNKS
    share = part // count_x
    rows = (members + 1) * nx + 8
    deep = rows + 8

    named = (obs_home[:, None] == jnp.arange(homes, dtype=jnp.int32)[None, :]).astype(jnp.int32)
    table = jnp.stack(
        [
            jnp.sum(named * (obs_line[:, None] + 1), axis=0),
            jnp.sum(named * obs_count[:, None], axis=0),
        ]
    ).astype(BF16)
    meta = jnp.pad(table, ((1, 13), (0, 128 - homes)))
    jt = jnp.transpose(jacobian[0])
    b, mine = pl.pallas_call(
        sensor_kernel,
        out_shape=(
            jax.ShapeDtypeStruct((2 * lev, channels), BF16),
            jax.ShapeDtypeStruct((homes, lev // 2 + 16, 2 * lev), BF16),
        ),
        in_specs=[vmem()] * 3,
        out_specs=(vmem(), vmem()),
        compiler_params=params(8),
        name="sensor",
    )(jt, obs_weight, meta)
    gathered = lax.all_to_all(mine, BOTH, split_axis=0, concat_axis=0, tiled=True)

    per = min(8, records)
    qs = pl.pallas_call(
        records_kernel,
        grid_spec=pltpu.PrefetchScalarGridSpec(
            num_scalar_prefetch=2,
            grid=(records // per,),
            in_specs=[
                pl.BlockSpec((2 * lev, channels), lambda i, *_: (0, 0)),
                pl.BlockSpec((per, channels, ny), lambda i, *_: (i, 0, 0)),
            ],
            out_specs=[pl.BlockSpec((homes, part, ny), lambda i, *_: (0, 0, 0))] * CHUNKS,
        ),
        out_shape=[jax.ShapeDtypeStruct((homes, part, ny), BF16)] * CHUNKS,
        compiler_params=params(56),
        name="records",
    )(obs_home, obs_count, b, departure)
    qs, wind_u, wind_v = lax.optimization_barrier((qs, wind_u, wind_v))
    before, after = wind_ends(wind_u, wind_v)
    qs, before, after = lax.optimization_barrier((qs, before, after))
    arrived = [lax.all_to_all(q, BOTH, split_axis=0, concat_axis=0, tiled=True) for q in qs]

    seen = lax.dynamic_slice_in_dim(
        gathered[:, lev // 2 + 1 : lev // 2 + 3, :], pos_x * count_y + pos_y, 1, axis=2
    )[:, :, 0].astype(jnp.int32)
    asked, counts = seen[:, 0], seen[:, 1]
    g1 = pl.pallas_call(
        columns_kernel,
        out_shape=jax.ShapeDtypeStruct((lev * nx, ny), F32),
        in_specs=[smem(), smem(), vmem(), vmem()],
        out_specs=vmem(),
        scratch_shapes=[pltpu.VMEM((lev * nx, ny), F32)],
        compiler_params=params(12),
        cost_estimate=pl.CostEstimate(flops=2**33, bytes_accessed=2**23, transcendentals=0),
        name="columns",
    )(asked, counts, gathered, increment).reshape(lev, nx, ny)
    select = (asked[:, None] == jnp.arange(1, nx + 1, dtype=jnp.int32)[None, :]).astype(BF16)

    length = filter_length
    fc = jnp.sqrt(-jnp.expm1(-2.0 / length))
    bc = -jnp.expm1(-1.0 / length)
    d = jnp.exp(-1.0 / length)

    def wide(columns, tail):
        got = jnp.stack(columns).reshape(len(columns), lev, *(1 for _ in tail))
        return jnp.broadcast_to(got, (len(columns), lev, *tail))

    coef_e = wide([d, fc, bc / fc, jnp.exp(-(nx + 1.0) / length), jnp.exp(1.0 / length)], (ny,))
    coef_f = wide([d, fc, bc], (ny,))
    jump, zero = jnp.exp(-nx / length), jnp.zeros_like(length)
    low = [entered(length, nx, float(i)) for i in range(3)]
    high = [entered(length, nx, float(nx - 3 + i)) for i in range(3)]
    low_b = [jnp.exp(-(nx - i) / length) for i in range(3)]
    high_b = [jnp.exp(-(3.0 - i) / length) for i in range(3)]
    kappa = entered(length, nx, 0.0)
    table_x = jnp.stack(
        [
            jnp.stack(line)
            for line in (
                [zero] * 3 + [jump] * 5,
                [jump] * 5 + [zero] * 3,
                [kappa] * 5 + [zero] * 3,
                low + [zero] * 5,
                low_b + [zero] * 5,
                [zero] * 5 + high,
                [zero] * 5 + high_b,
            )
        ]
    )
    table_x = jnp.transpose(table_x, (0, 2, 1))
    cells = jnp.arange(ny, dtype=F32)
    big = product(length[:, None, None], ny, cells[None, :, None], cells[None, None, :])
    nh, nl = split(big)
    edge = jnp.stack(
        [fc[:, None] * jnp.exp(-(ny - 1.0 - cells)[None] / length[:, None])]
        + [
            product(length[:, None], ny, float(i), cells[None, :])
            for i in (0, 1, 2, ny - 3, ny - 2, ny - 1)
        ]
        + [jnp.zeros((lev, ny), F32)],
        axis=1,
    )
    edge = jnp.concatenate(split(edge), axis=1)
    enter_a = entered(length[:, None], ny, cells[None, :])
    enter_b = jnp.exp(-(ny - cells)[None, :] / length[:, None])
    ah, al = split(enter_a)
    bh, bl = split(enter_b)
    none = jnp.zeros((lev, ny), BF16)
    place = jnp.stack([jnp.arange(ny) == k for k in (ny - 3, ny - 2, ny - 1, 0, 1, 2)]).astype(BF16)
    blank = jnp.zeros((8, ny), BF16)
    place = jnp.concatenate([blank, place, blank[:2]], axis=0)
    spread = jnp.concatenate(
        [
            jnp.stack([ah, ah, al, bh, bh, bl] + [none] * 10, axis=1),
            jnp.broadcast_to(place[None], (lev, 16, ny)),
        ],
        axis=2,
    )
    coef_y = wide(
        [jnp.exp(-ny / length), entered(length, ny, 0.0)]
        + [entered(length, ny, ny - 3.0 + i) for i in range(3)]
        + [jnp.exp(-(3.0 - i) / length) for i in range(3)]
        + [entered(length, ny, float(i)) for i in range(3)]
        + [jnp.exp(-(ny - float(i)) / length) for i in range(3)],
        (ny,),
    )
    sides = wind_sides(wind_u, wind_v, before, after)
    g1, *sides = lax.optimization_barrier((g1, *sides))
    halo_u, halo_v = padded_winds(wind_u, wind_v, (before, after, *sides))
    arrived, halo_u, halo_v, g1 = lax.optimization_barrier((arrived, halo_u, halo_v, g1))

    alpha = static = None
    for c in range(CHUNKS):
        g2 = jnp.einsum("sx,sly->lxy", select, arrived[c], preferred_element_type=F32)
        steps = part // 16
        off = c * steps
        h = pl.pallas_call(
            edges_kernel,
            grid=(steps,),
            in_specs=[
                pl.BlockSpec((16, nx, ny), lambda i, off=off: (off + i, 0, 0)),
                pl.BlockSpec((16, nx, ny), lambda i: (i, 0, 0)),
                pl.BlockSpec((members, 16, nx, ny), lambda i, off=off: (0, off + i, 0, 0)),
                pl.BlockSpec((5, 16, ny), lambda i, off=off: (0, off + i, 0)),
            ],
            out_specs=pl.BlockSpec((16, 16, ny), lambda i: (i, 0, 0)),
            out_shape=jax.ShapeDtypeStruct((part, 16, ny), F32),
            scratch_shapes=[pltpu.VMEM((16 * rows, ny), F32), pltpu.VMEM((16 * 16, ny), F32)],
            compiler_params=params(56),
            name=f"edges_{c}",
        )(g1, g2, ensemble, coef_e)
        h = lax.all_to_all(
            h.reshape(count_x, share, 16, ny), GX, split_axis=0, concat_axis=0, tiled=True
        )
        mine_x = lax.dynamic_slice_in_dim(table_x, c * part + pos_x * share, share, axis=1)
        mine_x = jnp.broadcast_to(mine_x[:, :, :, None], (7, share, 8, ny))
        h = pl.pallas_call(
            scan_x_kernel,
            out_shape=jax.ShapeDtypeStruct(h.shape, F32),
            in_specs=[vmem(), vmem()],
            out_specs=vmem(),
            compiler_params=params(8),
            name=f"scan_x_{c}",
        )(h, mine_x)
        h = lax.all_to_all(h, GX, split_axis=0, concat_axis=0, tiled=True).reshape(part, 16, ny)
        hi, lo, es, to_right, to_left = pl.pallas_call(
            filter_x_kernel,
            grid=(steps,),
            in_specs=[
                pl.BlockSpec((16, nx, ny), lambda i, off=off: (off + i, 0, 0)),
                pl.BlockSpec((16, nx, ny), lambda i: (i, 0, 0)),
                pl.BlockSpec((members, 16, nx, ny), lambda i, off=off: (0, off + i, 0, 0)),
                pl.BlockSpec((16, 16, ny), lambda i: (i, 0, 0)),
                pl.BlockSpec((3, 16, ny), lambda i, off=off: (0, off + i, 0)),
                pl.BlockSpec((16, 16, ny), lambda i, off=off: (off + i, 0, 0)),
            ],
            out_specs=(
                pl.BlockSpec((16, deep, ny), lambda i: (i, 0, 0)),
                pl.BlockSpec((16, deep, ny), lambda i: (i, 0, 0)),
                pl.BlockSpec((count_y, 2, 16, deep), lambda i: (0, 0, i, 0)),
                pl.BlockSpec((3, 16, ny), lambda i: (0, i, 0)),
                pl.BlockSpec((3, 16, ny), lambda i: (0, i, 0)),
            ),
            out_shape=(
                jax.ShapeDtypeStruct((part, deep, ny), BF16),
                jax.ShapeDtypeStruct((part, deep, ny), BF16),
                jax.ShapeDtypeStruct((count_y, 2, part, deep), BF16),
                jax.ShapeDtypeStruct((3, part, ny), BF16),
                jax.ShapeDtypeStruct((3, part, ny), BF16),
            ),
            scratch_shapes=[
                pltpu.VMEM((16 * rows, ny), F32),
                pltpu.VMEM((16 * (deep + 8), ny), F32),
                pltpu.VMEM((16 * 16, ny), F32),
                pltpu.VMEM((16 * 16, ny), F32),
            ],
            compiler_params=params(56),
            name=f"filter_x_{c}",
        )(g1, g2, ensemble, h, coef_f, edge)
        es = lax.all_to_all(es, GY, split_axis=0, concat_axis=0, tiled=True)
        from_left = from_before(to_right, GY)
        from_right = from_after(to_left, GY)
        fb = pl.pallas_call(
            scan_y_kernel,
            out_shape=jax.ShapeDtypeStruct((part * 16, deep), BF16),
            in_specs=[smem()] + [vmem()] * 4,
            out_specs=vmem(),
            scratch_shapes=[
                pltpu.VMEM((count_y, part, deep), F32),
                pltpu.VMEM((count_y, part, deep), F32),
                pltpu.VMEM((2, part * 16, deep // 2), F32),
            ],
            compiler_params=params(16),
            name=f"scan_y_{c}",
        )(pos_y.reshape(1), es, from_left, from_right, coef_y[:, c * part : (c + 1) * part])
        steps = part // 8
        off = c * steps
        extra = () if c == 0 else (alpha, static)
        alpha, static = pl.pallas_call(
            final_kernel,
            grid=(steps,),
            in_specs=[
                pl.BlockSpec((8, deep, ny), lambda i: (i, 0, 0)),
                pl.BlockSpec((8, deep, ny), lambda i: (i, 0, 0)),
                pl.BlockSpec((8, ny, ny), lambda i, off=off: (off + i, 0, 0)),
                pl.BlockSpec((8, ny, ny), lambda i, off=off: (off + i, 0, 0)),
                pl.BlockSpec((8 * 16, deep), lambda i: (i, 0)),
                pl.BlockSpec((8, 16, 2 * ny), lambda i, off=off: (off + i, 0, 0)),
                pl.BlockSpec((8, nx + 8, 2 * ny), lambda i, off=off: (off + i, 0, 0)),
                pl.BlockSpec((8, nx + 8, 2 * ny), lambda i, off=off: (off + i, 0, 0)),
            ]
            + [pl.BlockSpec(memory_space=pl.ANY)] * len(extra),
            out_specs=(
                pl.BlockSpec((members, 8, nx, ny), lambda i, off=off: (0, off + i, 0, 0)),
                pl.BlockSpec((8, nx, ny), lambda i, off=off: (off + i, 0, 0)),
            ),
            out_shape=(
                jax.ShapeDtypeStruct((members, lev, nx, ny), F32),
                jax.ShapeDtypeStruct((lev, nx, ny), F32),
            ),
            input_output_aliases={8: 0, 9: 1} if extra else {},
            compiler_params=params(56),
            name=f"final_{c}",
        )(hi, lo, nh, nl, fb, spread, halo_u, halo_v, *extra)
    return alpha, static


def solution(mesh):
    grid = P(None, GX, GY)
    placed = (
        grid,
        P(None, None, GX, GY),
        grid,
        grid,
        P(),
        P(BOTH, None, None),
        P(BOTH, None),
        P(BOTH, None, None),
        P(BOTH),
        P(BOTH),
        P(BOTH),
    )
    return jax.shard_map(
        body,
        mesh=mesh,
        in_specs=placed,
        out_specs=(P(None, None, GX, GY), grid),
        check_vma=False,
    )
```

```python
import functools

import jax
import jax.numpy as jnp
import numpy as np
from jax import lax
from jax.experimental import pallas as pl
from jax.experimental.pallas import tpu as pltpu
from jax.sharding import PartitionSpec as P

GX, GY = "gx", "gy"
BOTH = (GX, GY)
CHUNKS = 1
MIB = 2**20
F32, BF16 = jnp.float32, jnp.bfloat16

NT = (((1,), (1,)), ((), ()))
TN = (((0,), (0,)), ((), ()))


def vmem():
    return pl.BlockSpec(memory_space=pltpu.VMEM)


def smem():
    return pl.BlockSpec(memory_space=pltpu.SMEM)


def params(mib):
    return pltpu.CompilerParams(vmem_limit_bytes=mib * MIB)


def split(value):
    high = value.astype(BF16)
    return high, (value - high.astype(F32)).astype(BF16)


def sensor_kernel(jt_ref, w_ref, meta_ref, b_ref, out_ref):
    lev = jt_ref.shape[0]
    high, low = split(jt_ref[...].astype(F32) * w_ref[...])
    b_ref[:lev] = high
    b_ref[lev:] = low
    a = lax.dot_general(high, jt_ref[...], NT, preferred_element_type=F32)
    a += lax.dot_general(low, jt_ref[...], NT, preferred_element_type=F32)
    row = lax.broadcasted_iota(jnp.int32, a.shape, 0)
    col = lax.broadcasted_iota(jnp.int32, a.shape, 1)
    high = a.astype(BF16).astype(F32)
    packed = jnp.where(col >= row, high, a - high)
    diagonal = jnp.sum(jnp.where(col == row, a - high, 0.0), axis=0, keepdims=True)
    half = lev // 2
    packed = jnp.concatenate([packed[:half], packed[half:]], axis=1)
    meta = meta_ref[...].astype(F32)
    first = lax.broadcasted_iota(jnp.int32, meta.shape, 0) == 0
    meta = jnp.where(first, jnp.concatenate([diagonal, jnp.zeros_like(diagonal)], axis=1), meta)
    whole = jnp.concatenate([packed, meta], axis=0).astype(BF16)

    def copy(k, carry):
        out_ref[k] = whole
        return carry

    lax.fori_loop(0, out_ref.shape[0], copy, 0, unroll=8)


def records_kernel(home_ref, count_ref, b_ref, dep_ref, *outs):
    step, per = pl.program_id(0), dep_ref.shape[0]
    lev = b_ref.shape[0] // 2
    part = lev // len(outs)

    @pl.when(step == 0)
    def _():
        for out in outs:
            out[...] = jnp.zeros_like(out)

    lane = lax.broadcasted_iota(jnp.int32, (lev, dep_ref.shape[2]), 1)
    for k in range(per):
        both = jnp.dot(b_ref[...], dep_ref[k], preferred_element_type=F32)
        q = both[:lev] + both[lev:]
        q = jnp.where(lane < count_ref[step * per + k], q, 0.0).astype(BF16)
        for c, out in enumerate(outs):
            out[home_ref[step * per + k]] = q[c * part : (c + 1) * part]


def columns_kernel(line_ref, count_ref, gathered_ref, inc_ref, g_ref, x_ref):
    lev, nx, ny = inc_ref.shape
    for l in range(lev):
        x_ref[pl.ds(l * nx, nx), :] = inc_ref[l].astype(F32)
    g_ref[...] = jnp.zeros_like(g_ref)
    lane = lax.broadcasted_iota(jnp.int32, (lev, ny), 1)
    half = lev // 2
    eye = lax.broadcasted_iota(jnp.int32, (lev, lev), 0) == lax.broadcasted_iota(
        jnp.int32, (lev, lev), 1
    )
    group = 4

    def some(i, carry):
        found = []
        for k in range(group):
            s = i * group + k
            at = jnp.maximum(line_ref[s] - 1, 0)
            x = x_ref[pl.ds(at, lev, stride=nx), :].astype(BF16)
            kept = gathered_ref[s, :half].astype(F32)
            m = jnp.concatenate([kept[:, :lev], kept[:, lev:]], axis=0)
            diagonal = gathered_ref[s, half : half + 16].astype(F32)[:1, :lev]
            other = jnp.where(eye, diagonal, jnp.transpose(m))
            y = jnp.dot(
                jnp.concatenate([m, other], axis=1).astype(BF16),
                jnp.concatenate([x, x], axis=0),
                preferred_element_type=F32,
            )
            found.append((at, jnp.where(lane < count_ref[s], y, 0.0)))
        for at, y in found:
            g_ref[pl.ds(at, lev, stride=nx), :] += y
        return carry

    lax.fori_loop(0, line_ref.shape[0] // group, some, 0)


def lay_fields(g1_ref, g2_ref, ens_ref, f_ref):
    members, block, nx, ny = ens_ref.shape
    rows = (members + 1) * nx + 8
    for l in range(block):
        g = g1_ref[l] - g2_ref[l]
        f_ref[pl.ds(l * rows + members * nx, nx), :] = g
        for m in range(members):
            f_ref[pl.ds(l * rows + m * nx, nx), :] = ens_ref[m, l].astype(F32) * g


def edges_kernel(g1_ref, g2_ref, ens_ref, coef_ref, h_ref, f_ref, tmp_ref):
    members, block, nx, ny = ens_ref.shape
    fields = members + 1
    rows = fields * nx + 8
    lay_fields(g1_ref, g2_ref, ens_ref, f_ref)

    for base in range(0, block, 8):
        d, fc, rt, d49, inv = (coef_ref[k, base : base + 8] for k in range(5))

        def line(m, x, base=base):
            return f_ref[pl.ds(base * rows + m * nx + x, 8, stride=rows), :]

        ahead = [line(m, 0) for m in range(fields)]
        back = [line(m, nx - 1) for m in range(fields)]
        for x in range(1, nx):
            for m in range(fields):
                ahead[m] = d * ahead[m] + line(m, x)
                back[m] = d * back[m] + line(m, nx - 1 - x)

        def put(row, value, base=base):
            tmp_ref[pl.ds(base * 16 + row, 8, stride=16), :] = value

        for m in range(fields):
            put(3 + m, fc * ahead[m])
            put(8 + m, rt * (back[m] - d49 * ahead[m]))
        e, p = ahead[members], back[members]
        f0, f1 = line(members, 0), line(members, 1)
        f46, f47 = line(members, nx - 2), line(members, nx - 1)
        d48, d47 = d49 * inv, d49 * inv * inv
        p1 = (p - f0) * inv
        p2 = (p1 - f1) * inv
        put(0, rt * (p - d49 * e))
        put(1, rt * (d * f0 + p1 - d48 * e))
        put(2, rt * (d * (d * f0 + f1) + p2 - d47 * e))
        e1 = (e - f47) * inv
        e2 = (e1 - f46) * inv
        put(13, rt * (e2 + d * (f46 + d * f47) - d * d * d * d * e))
        put(14, rt * (e1 + d * f47 - d * d * d * e))
        put(15, rt * (e - d * d * e))
    for l in range(block):
        h_ref[l] = tmp_ref[pl.ds(l * 16, 16), :]


def scan_x_kernel(in_ref, coef_ref, out_ref):
    count, levels = in_ref.shape[:2]
    row = lax.broadcasted_iota(jnp.int32, (8, in_ref.shape[3]), 0)
    for l in range(levels):
        d0, d1, kappa, a0, b0, a1, b1 = (coef_ref[k, l] for k in range(7))
        first, second = [], []
        for g in range(count):
            v = in_ref[g, l].astype(F32)
            first.append(v[:8])
            second.append(v[8:])
        ahead = [jnp.zeros_like(row, F32)]
        for g in range(count - 1):
            ahead.append(first[g] + d0 * ahead[g])
        turned = [pltpu.roll(a, 5, 0) for a in ahead]
        back = [jnp.zeros_like(row, F32)] * count
        for g in range(count - 1, 0, -1):
            back[g - 1] = second[g] + kappa * turned[g] + d1 * back[g]
        static = [(ahead[g][7:8], back[g][4:5]) for g in range(count)]
        low = [first[g] + a0 * static[g][0] + b0 * static[g][1] for g in range(count)]
        high = [second[g] + a1 * static[g][0] + b1 * static[g][1] for g in range(count)]
        none = jnp.zeros_like(row, F32)
        for g in range(count):
            after = low[g + 1] if g + 1 < count else none
            before = high[g - 1] if g > 0 else none
            out_ref[g, l] = jnp.concatenate(
                [jnp.where(row < 3, after, ahead[g]), jnp.where(row < 5, back[g], before)], axis=0
            )


def filter_x_kernel(
    g1_ref,
    g2_ref,
    ens_ref,
    fb_ref,
    coef_ref,
    v_ref,
    hi_ref,
    lo_ref,
    es_ref,
    right_ref,
    left_ref,
    f_ref,
    xs_ref,
    st_ref,
    ey_ref,
):
    members, block, nx, _ = ens_ref.shape
    fields = members + 1
    used = fields * nx
    rows = used + 8
    lay_fields(g1_ref, g2_ref, ens_ref, f_ref)
    deep = hi_ref.shape[1]
    wide = deep + 8
    for l in range(block):
        st_ref[pl.ds(l * 16, 16), :] = fb_ref[l]
    for base in range(0, block, 8):
        d, fc, bc = (coef_ref[k, base : base + 8] for k in (0, 1, 5))

        def at(m, x, base=base):
            return pl.ds(base * wide + m * nx + x, 8, stride=wide)

        state = [st_ref[pl.ds(base * 16 + 3 + m, 8, stride=16), :] for m in range(fields)]
        for x in range(nx):
            for m in range(fields):
                f = f_ref[pl.ds(base * rows + m * nx + x, 8, stride=rows), :]
                state[m] = fc * f + d * state[m]
                xs_ref[at(m, x), :] = state[m]
        state = [st_ref[pl.ds(base * 16 + 8 + m, 8, stride=16), :] for m in range(fields)]
        for x in range(nx - 1, -1, -1):
            for m in range(fields):
                state[m] = bc * xs_ref[at(m, x), :] + d * state[m]
                xs_ref[at(m, x), :] = state[m]
    row = lax.broadcasted_iota(jnp.int32, (8, f_ref.shape[1]), 0)
    for l in range(block):
        after, before = st_ref[pl.ds(l * 16, 8), :], st_ref[pl.ds(l * 16 + 8, 8), :]
        halo = jnp.where(row < 3, after, jnp.where(row < 5, 0.0, before))
        xs_ref[pl.ds(l * wide + used, 8), :] = halo
        xs_ref[pl.ds(l * wide + used + 8, 8), :] = jnp.zeros_like(halo)
        hi, lo = split(xs_ref[pl.ds(l * wide, deep), :])
        hi_ref[l] = hi
        lo_ref[l] = lo
        one = lax.dot_general(v_ref[l], hi, NT, preferred_element_type=F32)
        two = lax.dot_general(v_ref[l], lo, NT, preferred_element_type=F32)
        ey_ref[pl.ds(l, 8, stride=block), :] = (one[:8] + one[8:] + two[:8])[:, : deep // 2]
        ey_ref[pl.ds(8 * block + l, 8, stride=block), :] = (one[:8] + one[8:] + two[:8])[
            :, deep // 2 :
        ]

    def both(q, side):
        return ey_ref[pl.ds((8 * side + q) * block, block), :].astype(BF16)

    for q in range(2):
        for side in range(2):
            got = both(q, side)
            lanes = pl.ds(side * got.shape[1], got.shape[1])
            for k in range(es_ref.shape[0]):
                es_ref[k, q, :, lanes] = got
    for q in range(3):
        left_ref[q] = both(1 + q, 1)
        right_ref[q] = both(4 + q, 1)


def scan_y_kernel(me_ref, es_ref, fl_ref, fr_ref, coef_ref, out_ref, ahead_ref, back_ref, tmp_ref):
    count, _, lev, lanes = es_ref.shape
    half = lanes // 2
    me = me_ref[0]
    decay, kappa = coef_ref[0], coef_ref[1]
    for side in range(2):
        part = pl.ds(side * half, half)
        state = jnp.zeros((lev, half), F32)
        ahead_ref[0, :, part] = state
        for k in range(count - 1):
            state = es_ref[k, 0, :, part].astype(F32) + decay * state
            ahead_ref[k + 1, :, part] = state
        state = jnp.zeros((lev, half), F32)
        back_ref[count - 1, :, part] = state
        for k in range(count - 1, 0, -1):
            state = (
                es_ref[k, 1, :, part].astype(F32)
                + kappa * ahead_ref[k, :, part]
                + decay * state
            )
            back_ref[k - 1, :, part] = state
    none = jnp.zeros((lev, half), F32)

    def put(q, side, value):
        tmp_ref[side, pl.ds(q, lev, stride=16), :] = value

    for side in range(2):
        part = pl.ds(side * half, half)
        for first, ref in ((0, ahead_ref), (3, back_ref)):
            value = ref[me, :, part]
            high = value.astype(BF16).astype(F32)
            put(first, side, high)
            put(first + 1, side, value - high)
            put(first + 2, side, high)
        for q in (6, 7, 14, 15):
            put(q, side, none)
    before, after = jnp.maximum(me - 1, 0), jnp.minimum(me + 1, count - 1)
    part = pl.ds(half, half)
    for q in range(3):
        put(8 + q, 0, none)
        put(11 + q, 0, none)
        value = (
            fl_ref[q].astype(F32)
            + coef_ref[2 + q] * ahead_ref[before, :, part]
            + coef_ref[5 + q] * back_ref[before, :, part]
        )
        put(8 + q, 1, jnp.where(me > 0, value, 0.0))
        value = (
            fr_ref[q].astype(F32)
            + coef_ref[8 + q] * ahead_ref[after, :, part]
            + coef_ref[11 + q] * back_ref[after, :, part]
        )
        put(11 + q, 1, jnp.where(me < count - 1, value, 0.0))
    for side in range(2):
        out_ref[:, pl.ds(side * half, half)] = tmp_ref[side].astype(BF16)


def final_kernel(hi_ref, lo_ref, nh_ref, nl_ref, fb_ref, ab_ref, u_ref, v_ref, *rest):
    alpha_ref, static_ref = rest[-2:]
    block = hi_ref.shape[0]
    members, _, nx, ny = alpha_ref.shape
    first = members * nx
    deep = nx + 8
    wide = 2 * ny
    for l in range(block):
        hi = hi_ref[l]
        more = lax.dot_general(
            fb_ref[pl.ds(l * 16, 16), :], ab_ref[l], TN, preferred_element_type=F32
        )
        got = jnp.dot(hi, nh_ref[l], preferred_element_type=F32)
        got += jnp.dot(hi, nl_ref[l], preferred_element_type=F32)
        got += jnp.dot(lo_ref[l], nh_ref[l], preferred_element_type=F32)
        got += more[:, :ny]
        for m in range(members):
            alpha_ref[m, l] = got[m * nx : (m + 1) * nx]
        s = jnp.concatenate(
            [got[first : first + deep], more[first : first + deep, ny:]], axis=1
        )
        u, v = u_ref[l].astype(F32), v_ref[l].astype(F32)
        up, vp = u > 0.0, v > 0.0
        u, v = jnp.abs(u), jnp.abs(v)
        for _ in range(3):
            s = s + u * (jnp.where(up, pltpu.roll(s, 1, 0), pltpu.roll(s, deep - 1, 0)) - s)
            s = s + v * (jnp.where(vp, pltpu.roll(s, 1, 1), pltpu.roll(s, wide - 1, 1)) - s)
        static_ref[l] = s[:nx, :ny]


def from_before(array, axis):
    count = lax.axis_size(axis)
    return lax.ppermute(array, axis, [(i, i + 1) for i in range(count - 1)])


def from_after(array, axis):
    count = lax.axis_size(axis)
    return lax.ppermute(array, axis, [(i + 1, i) for i in range(count - 1)])


def wind_rows_kernel(u_ref, v_ref, first_ref, last_ref):
    nx = u_ref.shape[1]
    for l in range(u_ref.shape[0]):
        u, v = u_ref[l].astype(F32), v_ref[l].astype(F32)
        first_ref[l] = jnp.concatenate([u[:8], v[:8]], axis=0).astype(BF16)
        last_ref[l] = jnp.concatenate([u[nx - 8 :], v[nx - 8 :]], axis=0).astype(BF16)


def taller(u_ref, v_ref, before_ref, after_ref, l):
    before, after = before_ref[l].astype(F32), after_ref[l].astype(F32)
    row = lax.broadcasted_iota(jnp.int32, (8, before.shape[1]), 0)
    both = []
    for k, ref in enumerate((u_ref, v_ref)):
        part = slice(8 * k, 8 * k + 8)
        halo = jnp.where(row < 3, after[part], jnp.where(row > 4, before[part], 0.0))
        both.append(jnp.concatenate([ref[l].astype(F32), halo], axis=0))
    return both


def wind_columns_kernel(u_ref, v_ref, before_ref, after_ref, pick_ref, right_ref, left_ref):
    for l in range(u_ref.shape[0]):
        u, v = taller(u_ref, v_ref, before_ref, after_ref, l)
        gap = jnp.zeros((8, u.shape[1]), F32)
        both = jnp.concatenate([u, gap, v, gap], axis=0).astype(BF16)
        got = lax.dot_general(pick_ref[...], both, NT, preferred_element_type=F32)
        half = got.shape[1] // 2
        for k, ref in enumerate((right_ref, left_ref)):
            some = got[8 * k : 8 * k + 8]
            ref[l] = jnp.concatenate([some[:, :half], some[:, half:]], axis=0).astype(BF16)


def wind_pad_kernel(
    u_ref, v_ref, before_ref, after_ref, left_ref, right_ref, place_ref, out_u_ref, out_v_ref
):
    ny = u_ref.shape[2]
    for l in range(u_ref.shape[0]):
        u, v = taller(u_ref, v_ref, before_ref, after_ref, l)
        sides = jnp.concatenate([left_ref[l], right_ref[l]], axis=0)
        got = lax.dot_general(sides, place_ref[...], TN, preferred_element_type=F32)[: len(u)]
        out_u_ref[l] = jnp.concatenate([u, got[:, :ny]], axis=1).astype(BF16)
        out_v_ref[l] = jnp.concatenate([v, got[:, ny:]], axis=1).astype(BF16)


def levels(*shape):
    return pl.BlockSpec((16, *shape), lambda i: (i, *(0 for _ in shape)))


def whole(*shape):
    return pl.BlockSpec(shape, lambda i: tuple(0 for _ in shape))


def wind_ends(wind_u, wind_v):
    lev, nx, ny = wind_u.shape
    steps = (lev // 16,)
    first, last = pl.pallas_call(
        wind_rows_kernel,
        grid=steps,
        in_specs=[levels(nx, ny)] * 2,
        out_specs=(levels(16, ny),) * 2,
        out_shape=(jax.ShapeDtypeStruct((lev, 16, ny), BF16),) * 2,
        compiler_params=params(8),
        name="wind_rows",
    )(wind_u, wind_v)
    return from_before(last, GX), from_after(first, GX)


def wind_sides(wind_u, wind_v, before, after):
    lev, nx, ny = wind_u.shape
    deep = nx + 16
    steps = (lev // 16,)
    pick = np.zeros((16, ny), np.float32)
    for k in range(3):
        pick[k, ny - 3 + k] = pick[8 + k, k] = 1
    right, left = pl.pallas_call(
        wind_columns_kernel,
        grid=steps,
        in_specs=[levels(nx, ny)] * 2 + [levels(16, ny)] * 2 + [whole(16, ny)],
        out_specs=(levels(16, deep),) * 2,
        out_shape=(jax.ShapeDtypeStruct((lev, 16, deep), BF16),) * 2,
        compiler_params=params(8),
        name="wind_columns",
    )(wind_u, wind_v, before, after, jnp.asarray(pick, BF16))
    return from_before(right, GY), from_after(left, GY)


def padded_winds(wind_u, wind_v, halos):
    lev, nx, ny = wind_u.shape
    deep = nx + 16
    place = np.zeros((32, 2 * ny), np.float32)
    for k in range(3):
        place[k, ny - 3 + k] = place[16 + k, k] = 1
        place[8 + k, 2 * ny - 3 + k] = place[24 + k, ny + k] = 1
    return pl.pallas_call(
        wind_pad_kernel,
        grid=(lev // 16,),
        in_specs=[levels(nx, ny)] * 2
        + [levels(16, ny)] * 2
        + [levels(16, deep)] * 2
        + [whole(32, 2 * ny)],
        out_specs=(levels(nx + 8, 2 * ny),) * 2,
        out_shape=(jax.ShapeDtypeStruct((lev, nx + 8, 2 * ny), BF16),) * 2,
        compiler_params=params(8),
        name="wind_pad",
    )(wind_u, wind_v, *halos, jnp.asarray(place, BF16))


def fell(z):
    near = z * (1.0 - z * (1.0 / 2 - z * (1.0 / 6 - z * (1.0 / 24 - z * (1.0 / 120 - z / 720)))))
    return jnp.where(z < 0.25, near, 1.0 - jnp.exp(-z))


def product(length, count, i, j):
    ratio = fell(1.0 / length) / jnp.sqrt(fell(2.0 / length))
    last = jnp.maximum(i, j)
    return ratio * jnp.exp(-jnp.abs(i - j) / length) * fell(2.0 * (count - last) / length)


def entered(length, count, i):
    ratio = fell(1.0 / length) / fell(2.0 / length)
    return ratio * jnp.exp(-(i + 1.0) / length) * fell(2.0 * (count - i) / length)


def tables_kernel(
    nx, share_ref, len_ref, wide_ref, e_ref, x_ref, v_ref, nh_ref, nl_ref, ab_ref, y_ref
):
    lev, ny, _ = nh_ref.shape
    length = wide_ref[...]
    fc, bc, d = jnp.sqrt(fell(2.0 / length)), fell(1.0 / length), jnp.exp(-1.0 / length)
    for k, value in enumerate(
        (d, fc, bc / fc, jnp.exp(-(nx + 1.0) / length), jnp.exp(1.0 / length), bc)
    ):
        e_ref[k] = value
    y_ref[0] = jnp.exp(-ny / length)
    y_ref[1] = entered(length, ny, 0.0)
    for i in range(3):
        y_ref[2 + i] = entered(length, ny, ny - 3.0 + i)
        y_ref[5 + i] = jnp.exp(-(3.0 - i) / length)
        y_ref[8 + i] = entered(length, ny, float(i))
        y_ref[11 + i] = jnp.exp(-(ny - float(i)) / length)

    row = lax.broadcasted_iota(jnp.int32, (8, ny), 0)
    at = row.astype(F32)
    top = row < 3
    for k in range(x_ref.shape[1]):
        own = jnp.full((8, ny), len_ref[share_ref[0] + k], F32)
        jump = jnp.exp(-nx / own)
        bottom = row > 4
        x_ref[0, k] = jnp.where(top, 0.0, jump)
        x_ref[1, k] = jnp.where(bottom, 0.0, jump)
        x_ref[2, k] = jnp.where(bottom, 0.0, entered(own, nx, 0.0))
        x_ref[3, k] = jnp.where(top, entered(own, nx, at), 0.0)
        x_ref[4, k] = jnp.where(top, jnp.exp(-(nx - at) / own), 0.0)
        x_ref[5, k] = jnp.where(bottom, entered(own, nx, nx - 8.0 + at), 0.0)
        x_ref[6, k] = jnp.where(bottom, jnp.exp(-(8.0 - at) / own), 0.0)

    cell = lax.broadcasted_iota(jnp.int32, (8, ny), 1)
    cells = cell.astype(F32)
    line = jnp.where(row < 4, at - 1.0, ny - 7.0 + at)
    zero = jnp.zeros((8, ny), F32)
    end, last = row < 3, row < 6
    lower = jnp.where(last & (cell == jnp.where(end, ny - 3 + row, row - 3)), 1.0, 0.0)
    place = jnp.concatenate([zero, lower], axis=0)
    across = lax.broadcasted_iota(jnp.int32, (ny, ny), 0).astype(F32)
    along = lax.broadcasted_iota(jnp.int32, (ny, ny), 1).astype(F32)
    apart, beyond = jnp.abs(across - along), ny - jnp.maximum(across, along)

    def level(l, carry):
        own = jnp.full((8, ny), len_ref[l], F32)
        root = jnp.sqrt(fell(2.0 / own))
        edge = jnp.where(
            row == 0, root * jnp.exp(-(ny - 1.0 - cells) / own), product(own, ny, line, cells)
        )
        high, low = split(jnp.where(row == 7, 0.0, edge))
        v_ref[l] = jnp.concatenate([high, low], axis=0)
        a, b = entered(own, ny, cells), jnp.exp(-(ny - cells) / own)
        part = jnp.where(end, a, b)
        high = part.astype(BF16).astype(F32)
        part = jnp.where((row == 2) | (row == 5), part - high, high)
        part = jnp.concatenate([jnp.where(last, part, 0.0), zero], axis=0)
        ab_ref[l] = jnp.concatenate([part, place], axis=1).astype(BF16)
        inverse = (1.0 / own)[:1]
        ratio = (fell(1.0 / own) / root)[:1]
        high, low = split(
            ratio * jnp.exp(-apart * inverse) * fell(2.0 * beyond * inverse)
        )
        nh_ref[l] = high
        nl_ref[l] = low
        return carry

    lax.fori_loop(0, lev, level, 0)


def body(
    increment,
    ensemble,
    wind_u,
    wind_v,
    filter_length,
    jacobian,
    obs_weight,
    departure,
    obs_home,
    obs_line,
    obs_count,
):
    count_x, count_y = lax.axis_size(GX), lax.axis_size(GY)
    homes = count_x * count_y
    pos_x, pos_y = lax.axis_index(GX), lax.axis_index(GY)
    lev, nx, ny = increment.shape
    members = ensemble.shape[0]
    channels = jacobian.shape[1]
    records = obs_home.shape[0]
    part = lev // CHUNKS
    share = part // count_x
    rows = (members + 1) * nx + 8
    deep = rows + 8

    named = (obs_home[:, None] == jnp.arange(homes, dtype=jnp.int32)[None, :]).astype(jnp.int32)
    table = jnp.stack(
        [
            jnp.sum(named * (obs_line[:, None] + 1), axis=0),
            jnp.sum(named * obs_count[:, None], axis=0),
        ]
    ).astype(BF16)
    meta = jnp.pad(table, ((1, 13), (0, 128 - homes)))
    jt = jnp.transpose(jacobian[0])
    b, mine = pl.pallas_call(
        sensor_kernel,
        out_shape=(
            jax.ShapeDtypeStruct((2 * lev, channels), BF16),
            jax.ShapeDtypeStruct((homes, lev // 2 + 16, 2 * lev), BF16),
        ),
        in_specs=[vmem()] * 3,
        out_specs=(vmem(), vmem()),
        compiler_params=params(8),
        name="sensor",
    )(jt, obs_weight, meta)
    gathered = lax.all_to_all(mine, BOTH, split_axis=0, concat_axis=0, tiled=True)

    per = min(8, records)
    qs = pl.pallas_call(
        records_kernel,
        grid_spec=pltpu.PrefetchScalarGridSpec(
            num_scalar_prefetch=2,
            grid=(records // per,),
            in_specs=[
                pl.BlockSpec((2 * lev, channels), lambda i, *_: (0, 0)),
                pl.BlockSpec((per, channels, ny), lambda i, *_: (i, 0, 0)),
            ],
            out_specs=[pl.BlockSpec((homes, part, ny), lambda i, *_: (0, 0, 0))] * CHUNKS,
        ),
        out_shape=[jax.ShapeDtypeStruct((homes, part, ny), BF16)] * CHUNKS,
        compiler_params=params(56),
        name="records",
    )(obs_home, obs_count, b, departure)
    qs, wind_u, wind_v = lax.optimization_barrier((qs, wind_u, wind_v))
    before, after = wind_ends(wind_u, wind_v)
    qs, before, after = lax.optimization_barrier((qs, before, after))
    arrived = [lax.all_to_all(q, BOTH, split_axis=0, concat_axis=0, tiled=True) for q in qs]

    seen = lax.dynamic_slice_in_dim(
        gathered[:, lev // 2 + 1 : lev // 2 + 3, :], pos_x * count_y + pos_y, 1, axis=2
    )[:, :, 0].astype(jnp.int32)
    asked, counts = seen[:, 0], seen[:, 1]
    g1 = pl.pallas_call(
        columns_kernel,
        out_shape=jax.ShapeDtypeStruct((lev * nx, ny), F32),
        in_specs=[smem(), smem(), vmem(), vmem()],
        out_specs=vmem(),
        scratch_shapes=[pltpu.VMEM((lev * nx, ny), F32)],
        compiler_params=params(12),
        cost_estimate=pl.CostEstimate(flops=2**33, bytes_accessed=2**23, transcendentals=0),
        name="columns",
    )(asked, counts, gathered, increment).reshape(lev, nx, ny)
    select = (asked[:, None] == jnp.arange(1, nx + 1, dtype=jnp.int32)[None, :]).astype(BF16)

    coef, table_x, edge, nh, nl, spread, coef_y = pl.pallas_call(
        functools.partial(tables_kernel, nx),
        out_shape=(
            jax.ShapeDtypeStruct((6, lev, ny), F32),
            jax.ShapeDtypeStruct((7, share, 8, ny), F32),
            jax.ShapeDtypeStruct((lev, 16, ny), BF16),
            jax.ShapeDtypeStruct((lev, ny, ny), BF16),
            jax.ShapeDtypeStruct((lev, ny, ny), BF16),
            jax.ShapeDtypeStruct((lev, 16, 2 * ny), BF16),
            jax.ShapeDtypeStruct((14, lev, ny), F32),
        ),
        in_specs=[smem(), smem(), vmem()],
        out_specs=(vmem(),) * 7,
        compiler_params=params(12),
        name="tables",
    )(
        (pos_x * share).reshape(1),
        filter_length,
        jnp.broadcast_to(filter_length[:, None], (lev, ny)),
    )
    sides = wind_sides(wind_u, wind_v, before, after)
    g1, *sides = lax.optimization_barrier((g1, *sides))
    halo_u, halo_v = padded_winds(wind_u, wind_v, (before, after, *sides))
    arrived, halo_u, halo_v, g1 = lax.optimization_barrier((arrived, halo_u, halo_v, g1))

    alpha = static = None
    for c in range(CHUNKS):
        g2 = jnp.einsum("sx,sly->lxy", select, arrived[c], preferred_element_type=F32)
        steps = part // 16
        off = c * steps
        h = pl.pallas_call(
            edges_kernel,
            grid=(steps,),
            in_specs=[
                pl.BlockSpec((16, nx, ny), lambda i, off=off: (off + i, 0, 0)),
                pl.BlockSpec((16, nx, ny), lambda i: (i, 0, 0)),
                pl.BlockSpec((members, 16, nx, ny), lambda i, off=off: (0, off + i, 0, 0)),
                pl.BlockSpec((6, 16, ny), lambda i, off=off: (0, off + i, 0)),
            ],
            out_specs=pl.BlockSpec((16, 16, ny), lambda i: (i, 0, 0)),
            out_shape=jax.ShapeDtypeStruct((part, 16, ny), F32),
            scratch_shapes=[pltpu.VMEM((16 * rows, ny), F32), pltpu.VMEM((16 * 16, ny), F32)],
            compiler_params=params(56),
            name=f"edges_{c}",
        )(g1, g2, ensemble, coef)
        h = lax.all_to_all(
            h.reshape(count_x, share, 16, ny), GX, split_axis=0, concat_axis=0, tiled=True
        )
        h = pl.pallas_call(
            scan_x_kernel,
            out_shape=jax.ShapeDtypeStruct(h.shape, F32),
            in_specs=[vmem(), vmem()],
            out_specs=vmem(),
            compiler_params=params(8),
            name=f"scan_x_{c}",
        )(h, table_x)
        h = lax.all_to_all(h, GX, split_axis=0, concat_axis=0, tiled=True).reshape(part, 16, ny)
        hi, lo, es, to_right, to_left = pl.pallas_call(
            filter_x_kernel,
            grid=(steps,),
            in_specs=[
                pl.BlockSpec((16, nx, ny), lambda i, off=off: (off + i, 0, 0)),
                pl.BlockSpec((16, nx, ny), lambda i: (i, 0, 0)),
                pl.BlockSpec((members, 16, nx, ny), lambda i, off=off: (0, off + i, 0, 0)),
                pl.BlockSpec((16, 16, ny), lambda i: (i, 0, 0)),
                pl.BlockSpec((6, 16, ny), lambda i, off=off: (0, off + i, 0)),
                pl.BlockSpec((16, 16, ny), lambda i, off=off: (off + i, 0, 0)),
            ],
            out_specs=(
                pl.BlockSpec((16, deep, ny), lambda i: (i, 0, 0)),
                pl.BlockSpec((16, deep, ny), lambda i: (i, 0, 0)),
                pl.BlockSpec((count_y, 2, 16, deep), lambda i: (0, 0, i, 0)),
                pl.BlockSpec((3, 16, ny), lambda i: (0, i, 0)),
                pl.BlockSpec((3, 16, ny), lambda i: (0, i, 0)),
            ),
            out_shape=(
                jax.ShapeDtypeStruct((part, deep, ny), BF16),
                jax.ShapeDtypeStruct((part, deep, ny), BF16),
                jax.ShapeDtypeStruct((count_y, 2, part, deep), BF16),
                jax.ShapeDtypeStruct((3, part, ny), BF16),
                jax.ShapeDtypeStruct((3, part, ny), BF16),
            ),
            scratch_shapes=[
                pltpu.VMEM((16 * rows, ny), F32),
                pltpu.VMEM((16 * (deep + 8), ny), F32),
                pltpu.VMEM((16 * 16, ny), F32),
                pltpu.VMEM((16 * 16, ny), F32),
            ],
            compiler_params=params(56),
            name=f"filter_x_{c}",
        )(g1, g2, ensemble, h, coef, edge)
        es = lax.all_to_all(es, GY, split_axis=0, concat_axis=0, tiled=True)
        from_left = from_before(to_right, GY)
        from_right = from_after(to_left, GY)
        fb = pl.pallas_call(
            scan_y_kernel,
            out_shape=jax.ShapeDtypeStruct((part * 16, deep), BF16),
            in_specs=[smem()] + [vmem()] * 4,
            out_specs=vmem(),
            scratch_shapes=[
                pltpu.VMEM((count_y, part, deep), F32),
                pltpu.VMEM((count_y, part, deep), F32),
                pltpu.VMEM((2, part * 16, deep // 2), F32),
            ],
            compiler_params=params(16),
            name=f"scan_y_{c}",
        )(pos_y.reshape(1), es, from_left, from_right, coef_y[:, c * part : (c + 1) * part])
        steps = part // 8
        off = c * steps
        extra = () if c == 0 else (alpha, static)
        alpha, static = pl.pallas_call(
            final_kernel,
            grid=(steps,),
            in_specs=[
                pl.BlockSpec((8, deep, ny), lambda i: (i, 0, 0)),
                pl.BlockSpec((8, deep, ny), lambda i: (i, 0, 0)),
                pl.BlockSpec((8, ny, ny), lambda i, off=off: (off + i, 0, 0)),
                pl.BlockSpec((8, ny, ny), lambda i, off=off: (off + i, 0, 0)),
                pl.BlockSpec((8 * 16, deep), lambda i: (i, 0)),
                pl.BlockSpec((8, 16, 2 * ny), lambda i, off=off: (off + i, 0, 0)),
                pl.BlockSpec((8, nx + 8, 2 * ny), lambda i, off=off: (off + i, 0, 0)),
                pl.BlockSpec((8, nx + 8, 2 * ny), lambda i, off=off: (off + i, 0, 0)),
            ]
            + [pl.BlockSpec(memory_space=pl.ANY)] * len(extra),
            out_specs=(
                pl.BlockSpec((members, 8, nx, ny), lambda i, off=off: (0, off + i, 0, 0)),
                pl.BlockSpec((8, nx, ny), lambda i, off=off: (off + i, 0, 0)),
            ),
            out_shape=(
                jax.ShapeDtypeStruct((members, lev, nx, ny), F32),
                jax.ShapeDtypeStruct((lev, nx, ny), F32),
            ),
            input_output_aliases={8: 0, 9: 1} if extra else {},
            compiler_params=params(56),
            name=f"final_{c}",
        )(hi, lo, nh, nl, fb, spread, halo_u, halo_v, *extra)
    return alpha, static


def solution(mesh):
    grid = P(None, GX, GY)
    placed = (
        grid,
        P(None, None, GX, GY),
        grid,
        grid,
        P(),
        P(BOTH, None, None),
        P(BOTH, None),
        P(BOTH, None, None),
        P(BOTH),
        P(BOTH),
        P(BOTH),
    )
    return jax.shard_map(
        body,
        mesh=mesh,
        in_specs=placed,
        out_specs=(P(None, None, GX, GY), grid),
        check_vma=False,
    )
```

```python
import functools

import jax
import jax.numpy as jnp
import numpy as np
from jax import lax
from jax.experimental import pallas as pl
from jax.experimental.pallas import tpu as pltpu
from jax.sharding import PartitionSpec as P

GX, GY = "gx", "gy"
BOTH = (GX, GY)
CHUNKS = 1
MIB = 2**20
F32, BF16 = jnp.float32, jnp.bfloat16

NT = (((1,), (1,)), ((), ()))
TN = (((0,), (0,)), ((), ()))


def vmem():
    return pl.BlockSpec(memory_space=pltpu.VMEM)


def smem():
    return pl.BlockSpec(memory_space=pltpu.SMEM)


def params(mib):
    return pltpu.CompilerParams(vmem_limit_bytes=mib * MIB)


def split(value):
    high = value.astype(BF16)
    return high, (value - high.astype(F32)).astype(BF16)


def sensor_kernel(jt_ref, w_ref, meta_ref, b_ref, out_ref):
    lev = jt_ref.shape[0]
    high, low = split(jt_ref[...].astype(F32) * w_ref[...])
    b_ref[:lev] = high
    b_ref[lev:] = low
    a = lax.dot_general(high, jt_ref[...], NT, preferred_element_type=F32)
    a += lax.dot_general(low, jt_ref[...], NT, preferred_element_type=F32)
    row = lax.broadcasted_iota(jnp.int32, a.shape, 0)
    col = lax.broadcasted_iota(jnp.int32, a.shape, 1)
    high = a.astype(BF16).astype(F32)
    packed = jnp.where(col >= row, high, a - high)
    diagonal = jnp.sum(jnp.where(col == row, a - high, 0.0), axis=0, keepdims=True)
    half = lev // 2
    packed = jnp.concatenate([packed[:half], packed[half:]], axis=1)
    meta = meta_ref[...].astype(F32)
    first = lax.broadcasted_iota(jnp.int32, meta.shape, 0) == 0
    meta = jnp.where(first, jnp.concatenate([diagonal, jnp.zeros_like(diagonal)], axis=1), meta)
    whole = jnp.concatenate([packed, meta], axis=0).astype(BF16)

    def copy(k, carry):
        out_ref[k] = whole
        return carry

    lax.fori_loop(0, out_ref.shape[0], copy, 0, unroll=8)


def records_kernel(home_ref, count_ref, b_ref, dep_ref, *outs):
    step, per = pl.program_id(0), dep_ref.shape[0]
    lev = b_ref.shape[0] // 2
    part = lev // len(outs)

    @pl.when(step == 0)
    def _():
        for out in outs:
            out[...] = jnp.zeros_like(out)

    lane = lax.broadcasted_iota(jnp.int32, (lev, dep_ref.shape[2]), 1)
    for k in range(per):
        both = jnp.dot(b_ref[...], dep_ref[k], preferred_element_type=F32)
        q = both[:lev] + both[lev:]
        q = jnp.where(lane < count_ref[step * per + k], q, 0.0).astype(BF16)
        for c, out in enumerate(outs):
            out[home_ref[step * per + k]] = q[c * part : (c + 1) * part]


def columns_kernel(line_ref, count_ref, gathered_ref, inc_ref, g_ref, x_ref):
    lev, nx, ny = inc_ref.shape
    for l in range(lev):
        x_ref[pl.ds(l * nx, nx), :] = inc_ref[l].astype(F32)
    g_ref[...] = jnp.zeros_like(g_ref)
    lane = lax.broadcasted_iota(jnp.int32, (lev, ny), 1)
    half = lev // 2
    eye = lax.broadcasted_iota(jnp.int32, (lev, lev), 0) == lax.broadcasted_iota(
        jnp.int32, (lev, lev), 1
    )
    group = 4

    def some(i, carry):
        found = []
        for k in range(group):
            s = i * group + k
            at = jnp.maximum(line_ref[s] - 1, 0)
            x = x_ref[pl.ds(at, lev, stride=nx), :].astype(BF16)
            kept = gathered_ref[s, :half].astype(F32)
            m = jnp.concatenate([kept[:, :lev], kept[:, lev:]], axis=0)
            diagonal = gathered_ref[s, half : half + 16].astype(F32)[:1, :lev]
            other = jnp.where(eye, diagonal, jnp.transpose(m))
            y = jnp.dot(
                jnp.concatenate([m, other], axis=1).astype(BF16),
                jnp.concatenate([x, x], axis=0),
                preferred_element_type=F32,
            )
            found.append((at, jnp.where(lane < count_ref[s], y, 0.0)))
        for at, y in found:
            g_ref[pl.ds(at, lev, stride=nx), :] += y
        return carry

    lax.fori_loop(0, line_ref.shape[0] // group, some, 0)


def lay_fields(g1_ref, g2_ref, ens_ref, f_ref):
    members, block, nx, ny = ens_ref.shape
    rows = (members + 1) * nx + 8
    for l in range(block):
        g = g1_ref[l] - g2_ref[l]
        f_ref[pl.ds(l * rows + members * nx, nx), :] = g
        for m in range(members):
            f_ref[pl.ds(l * rows + m * nx, nx), :] = ens_ref[m, l].astype(F32) * g


def edges_kernel(g1_ref, g2_ref, ens_ref, coef_ref, h_ref, f_ref, tmp_ref):
    members, block, nx, ny = ens_ref.shape
    fields = members + 1
    rows = fields * nx + 8
    lay_fields(g1_ref, g2_ref, ens_ref, f_ref)

    for base in range(0, block, 8):
        d, fc, rt, d49, inv = (coef_ref[k, base : base + 8] for k in range(5))

        def line(m, x, base=base):
            return f_ref[pl.ds(base * rows + m * nx + x, 8, stride=rows), :]

        ahead = [line(m, 0) for m in range(fields)]
        back = [line(m, nx - 1) for m in range(fields)]
        for x in range(1, nx):
            for m in range(fields):
                ahead[m] = d * ahead[m] + line(m, x)
                back[m] = d * back[m] + line(m, nx - 1 - x)

        def put(row, value, base=base):
            tmp_ref[pl.ds(base * 16 + row, 8, stride=16), :] = value

        for m in range(fields):
            put(3 + m, fc * ahead[m])
            put(8 + m, rt * (back[m] - d49 * ahead[m]))
        e, p = ahead[members], back[members]
        f0, f1 = line(members, 0), line(members, 1)
        f46, f47 = line(members, nx - 2), line(members, nx - 1)
        d48, d47 = d49 * inv, d49 * inv * inv
        p1 = (p - f0) * inv
        p2 = (p1 - f1) * inv
        put(0, rt * (p - d49 * e))
        put(1, rt * (d * f0 + p1 - d48 * e))
        put(2, rt * (d * (d * f0 + f1) + p2 - d47 * e))
        e1 = (e - f47) * inv
        e2 = (e1 - f46) * inv
        put(13, rt * (e2 + d * (f46 + d * f47) - d * d * d * d * e))
        put(14, rt * (e1 + d * f47 - d * d * d * e))
        put(15, rt * (e - d * d * e))
    for l in range(block):
        h_ref[l] = tmp_ref[pl.ds(l * 16, 16), :].astype(BF16)


def scan_x_kernel(in_ref, coef_ref, out_ref):
    count, levels = in_ref.shape[:2]
    row = lax.broadcasted_iota(jnp.int32, (8, in_ref.shape[3]), 0)
    for l in range(levels):
        d0, d1, kappa, a0, b0, a1, b1 = (coef_ref[k, l] for k in range(7))
        first, second = [], []
        for g in range(count):
            v = in_ref[g, l].astype(F32)
            first.append(v[:8])
            second.append(v[8:])
        ahead = [jnp.zeros_like(row, F32)]
        for g in range(count - 1):
            ahead.append(first[g] + d0 * ahead[g])
        turned = [pltpu.roll(a, 5, 0) for a in ahead]
        back = [jnp.zeros_like(row, F32)] * count
        for g in range(count - 1, 0, -1):
            back[g - 1] = second[g] + kappa * turned[g] + d1 * back[g]
        static = [(ahead[g][7:8], back[g][4:5]) for g in range(count)]
        low = [first[g] + a0 * static[g][0] + b0 * static[g][1] for g in range(count)]
        high = [second[g] + a1 * static[g][0] + b1 * static[g][1] for g in range(count)]
        none = jnp.zeros_like(row, F32)
        for g in range(count):
            after = low[g + 1] if g + 1 < count else none
            before = high[g - 1] if g > 0 else none
            out_ref[g, l] = jnp.concatenate(
                [jnp.where(row < 3, after, ahead[g]), jnp.where(row < 5, back[g], before)], axis=0
            ).astype(BF16)


def filter_x_kernel(
    g1_ref,
    g2_ref,
    ens_ref,
    fb_ref,
    coef_ref,
    v_ref,
    hi_ref,
    lo_ref,
    es_ref,
    right_ref,
    left_ref,
    f_ref,
    xs_ref,
    st_ref,
    ey_ref,
):
    members, block, nx, _ = ens_ref.shape
    fields = members + 1
    used = fields * nx
    rows = used + 8
    lay_fields(g1_ref, g2_ref, ens_ref, f_ref)
    deep = hi_ref.shape[1]
    wide = deep + 8
    for l in range(block):
        st_ref[pl.ds(l * 16, 16), :] = fb_ref[l].astype(F32)
    for base in range(0, block, 8):
        d, fc, bc = (coef_ref[k, base : base + 8] for k in (0, 1, 5))

        def at(m, x, base=base):
            return pl.ds(base * wide + m * nx + x, 8, stride=wide)

        state = [st_ref[pl.ds(base * 16 + 3 + m, 8, stride=16), :] for m in range(fields)]
        for x in range(nx):
            for m in range(fields):
                f = f_ref[pl.ds(base * rows + m * nx + x, 8, stride=rows), :]
                state[m] = fc * f + d * state[m]
                xs_ref[at(m, x), :] = state[m]
        state = [st_ref[pl.ds(base * 16 + 8 + m, 8, stride=16), :] for m in range(fields)]
        for x in range(nx - 1, -1, -1):
            for m in range(fields):
                state[m] = bc * xs_ref[at(m, x), :] + d * state[m]
                xs_ref[at(m, x), :] = state[m]
    row = lax.broadcasted_iota(jnp.int32, (8, f_ref.shape[1]), 0)
    for l in range(block):
        after, before = st_ref[pl.ds(l * 16, 8), :], st_ref[pl.ds(l * 16 + 8, 8), :]
        halo = jnp.where(row < 3, after, jnp.where(row < 5, 0.0, before))
        xs_ref[pl.ds(l * wide + used, 8), :] = halo
        xs_ref[pl.ds(l * wide + used + 8, 8), :] = jnp.zeros_like(halo)
        hi, lo = split(xs_ref[pl.ds(l * wide, deep), :])
        hi_ref[l] = hi
        lo_ref[l] = lo
        one = lax.dot_general(v_ref[l], hi, NT, preferred_element_type=F32)
        two = lax.dot_general(v_ref[l], lo, NT, preferred_element_type=F32)
        ey_ref[pl.ds(l, 8, stride=block), :] = (one[:8] + one[8:] + two[:8])[:, : deep // 2]
        ey_ref[pl.ds(8 * block + l, 8, stride=block), :] = (one[:8] + one[8:] + two[:8])[
            :, deep // 2 :
        ]

    def both(q, side):
        return ey_ref[pl.ds((8 * side + q) * block, block), :].astype(BF16)

    for q in range(2):
        for side in range(2):
            got = both(q, side)
            lanes = pl.ds(side * got.shape[1], got.shape[1])
            for k in range(es_ref.shape[0]):
                es_ref[k, q, :, lanes] = got
    for q in range(3):
        left_ref[q] = both(1 + q, 1)
        right_ref[q] = both(4 + q, 1)


def scan_y_kernel(me_ref, es_ref, fl_ref, fr_ref, coef_ref, out_ref, ahead_ref, back_ref, tmp_ref):
    count, _, lev, lanes = es_ref.shape
    half = lanes // 2
    me = me_ref[0]
    decay, kappa = coef_ref[0], coef_ref[1]
    for side in range(2):
        part = pl.ds(side * half, half)
        state = jnp.zeros((lev, half), F32)
        ahead_ref[0, :, part] = state
        for k in range(count - 1):
            state = es_ref[k, 0, :, part].astype(F32) + decay * state
            ahead_ref[k + 1, :, part] = state
        state = jnp.zeros((lev, half), F32)
        back_ref[count - 1, :, part] = state
        for k in range(count - 1, 0, -1):
            state = (
                es_ref[k, 1, :, part].astype(F32)
                + kappa * ahead_ref[k, :, part]
                + decay * state
            )
            back_ref[k - 1, :, part] = state
    none = jnp.zeros((lev, half), F32)

    def put(q, side, value):
        tmp_ref[side, pl.ds(q, lev, stride=16), :] = value

    for side in range(2):
        part = pl.ds(side * half, half)
        for first, ref in ((0, ahead_ref), (3, back_ref)):
            value = ref[me, :, part]
            high = value.astype(BF16).astype(F32)
            put(first, side, high)
            put(first + 1, side, value - high)
            put(first + 2, side, high)
        for q in (6, 7, 14, 15):
            put(q, side, none)
    before, after = jnp.maximum(me - 1, 0), jnp.minimum(me + 1, count - 1)
    part = pl.ds(half, half)
    for q in range(3):
        put(8 + q, 0, none)
        put(11 + q, 0, none)
        value = (
            fl_ref[q].astype(F32)
            + coef_ref[2 + q] * ahead_ref[before, :, part]
            + coef_ref[5 + q] * back_ref[before, :, part]
        )
        put(8 + q, 1, jnp.where(me > 0, value, 0.0))
        value = (
            fr_ref[q].astype(F32)
            + coef_ref[8 + q] * ahead_ref[after, :, part]
            + coef_ref[11 + q] * back_ref[after, :, part]
        )
        put(11 + q, 1, jnp.where(me < count - 1, value, 0.0))
    for side in range(2):
        out_ref[:, pl.ds(side * half, half)] = tmp_ref[side].astype(BF16)


def final_kernel(hi_ref, lo_ref, nh_ref, nl_ref, fb_ref, ab_ref, u_ref, v_ref, *rest):
    alpha_ref, static_ref = rest[-2:]
    block = hi_ref.shape[0]
    members, _, nx, ny = alpha_ref.shape
    first = members * nx
    deep = nx + 8
    wide = 2 * ny
    for l in range(block):
        hi = hi_ref[l]
        more = lax.dot_general(
            fb_ref[pl.ds(l * 16, 16), :], ab_ref[l], TN, preferred_element_type=F32
        )
        got = jnp.dot(hi, nh_ref[l], preferred_element_type=F32)
        got += jnp.dot(hi, nl_ref[l], preferred_element_type=F32)
        got += jnp.dot(lo_ref[l], nh_ref[l], preferred_element_type=F32)
        got += more[:, :ny]
        for m in range(members):
            alpha_ref[m, l] = got[m * nx : (m + 1) * nx]
        s = jnp.concatenate(
            [got[first : first + deep], more[first : first + deep, ny:]], axis=1
        )
        u, v = u_ref[l].astype(F32), v_ref[l].astype(F32)
        up, vp = u > 0.0, v > 0.0
        u, v = jnp.abs(u), jnp.abs(v)
        for _ in range(3):
            s = s + u * (jnp.where(up, pltpu.roll(s, 1, 0), pltpu.roll(s, deep - 1, 0)) - s)
            s = s + v * (jnp.where(vp, pltpu.roll(s, 1, 1), pltpu.roll(s, wide - 1, 1)) - s)
        static_ref[l] = s[:nx, :ny]


def from_before(array, axis):
    count = lax.axis_size(axis)
    return lax.ppermute(array, axis, [(i, i + 1) for i in range(count - 1)])


def from_after(array, axis):
    count = lax.axis_size(axis)
    return lax.ppermute(array, axis, [(i + 1, i) for i in range(count - 1)])


def wind_rows_kernel(u_ref, v_ref, first_ref, last_ref):
    nx = u_ref.shape[1]
    for l in range(u_ref.shape[0]):
        u, v = u_ref[l].astype(F32), v_ref[l].astype(F32)
        first_ref[l] = jnp.concatenate([u[:8], v[:8]], axis=0).astype(BF16)
        last_ref[l] = jnp.concatenate([u[nx - 8 :], v[nx - 8 :]], axis=0).astype(BF16)


def taller(u_ref, v_ref, before_ref, after_ref, l):
    before, after = before_ref[l].astype(F32), after_ref[l].astype(F32)
    row = lax.broadcasted_iota(jnp.int32, (8, before.shape[1]), 0)
    both = []
    for k, ref in enumerate((u_ref, v_ref)):
        part = slice(8 * k, 8 * k + 8)
        halo = jnp.where(row < 3, after[part], jnp.where(row > 4, before[part], 0.0))
        both.append(jnp.concatenate([ref[l].astype(F32), halo], axis=0))
    return both


def wind_columns_kernel(u_ref, v_ref, before_ref, after_ref, pick_ref, right_ref, left_ref):
    for l in range(u_ref.shape[0]):
        u, v = taller(u_ref, v_ref, before_ref, after_ref, l)
        gap = jnp.zeros((8, u.shape[1]), F32)
        both = jnp.concatenate([u, gap, v, gap], axis=0).astype(BF16)
        got = lax.dot_general(pick_ref[...], both, NT, preferred_element_type=F32)
        half = got.shape[1] // 2
        for k, ref in enumerate((right_ref, left_ref)):
            some = got[8 * k : 8 * k + 8]
            ref[l] = jnp.concatenate([some[:, :half], some[:, half:]], axis=0).astype(BF16)


def wind_pad_kernel(
    u_ref, v_ref, before_ref, after_ref, left_ref, right_ref, place_ref, out_u_ref, out_v_ref
):
    ny = u_ref.shape[2]
    for l in range(u_ref.shape[0]):
        u, v = taller(u_ref, v_ref, before_ref, after_ref, l)
        sides = jnp.concatenate([left_ref[l], right_ref[l]], axis=0)
        got = lax.dot_general(sides, place_ref[...], TN, preferred_element_type=F32)[: len(u)]
        out_u_ref[l] = jnp.concatenate([u, got[:, :ny]], axis=1).astype(BF16)
        out_v_ref[l] = jnp.concatenate([v, got[:, ny:]], axis=1).astype(BF16)


def levels(*shape):
    return pl.BlockSpec((16, *shape), lambda i: (i, *(0 for _ in shape)))


def whole(*shape):
    return pl.BlockSpec(shape, lambda i: tuple(0 for _ in shape))


def wind_ends(wind_u, wind_v):
    lev, nx, ny = wind_u.shape
    steps = (lev // 16,)
    first, last = pl.pallas_call(
        wind_rows_kernel,
        grid=steps,
        in_specs=[levels(nx, ny)] * 2,
        out_specs=(levels(16, ny),) * 2,
        out_shape=(jax.ShapeDtypeStruct((lev, 16, ny), BF16),) * 2,
        compiler_params=params(8),
        name="wind_rows",
    )(wind_u, wind_v)
    return from_before(last, GX), from_after(first, GX)


def wind_sides(wind_u, wind_v, before, after):
    lev, nx, ny = wind_u.shape
    deep = nx + 16
    steps = (lev // 16,)
    pick = np.zeros((16, ny), np.float32)
    for k in range(3):
        pick[k, ny - 3 + k] = pick[8 + k, k] = 1
    right, left = pl.pallas_call(
        wind_columns_kernel,
        grid=steps,
        in_specs=[levels(nx, ny)] * 2 + [levels(16, ny)] * 2 + [whole(16, ny)],
        out_specs=(levels(16, deep),) * 2,
        out_shape=(jax.ShapeDtypeStruct((lev, 16, deep), BF16),) * 2,
        compiler_params=params(8),
        name="wind_columns",
    )(wind_u, wind_v, before, after, jnp.asarray(pick, BF16))
    return from_before(right, GY), from_after(left, GY)


def padded_winds(wind_u, wind_v, halos):
    lev, nx, ny = wind_u.shape
    deep = nx + 16
    place = np.zeros((32, 2 * ny), np.float32)
    for k in range(3):
        place[k, ny - 3 + k] = place[16 + k, k] = 1
        place[8 + k, 2 * ny - 3 + k] = place[24 + k, ny + k] = 1
    return pl.pallas_call(
        wind_pad_kernel,
        grid=(lev // 16,),
        in_specs=[levels(nx, ny)] * 2
        + [levels(16, ny)] * 2
        + [levels(16, deep)] * 2
        + [whole(32, 2 * ny)],
        out_specs=(levels(nx + 8, 2 * ny),) * 2,
        out_shape=(jax.ShapeDtypeStruct((lev, nx + 8, 2 * ny), BF16),) * 2,
        compiler_params=params(8),
        name="wind_pad",
    )(wind_u, wind_v, *halos, jnp.asarray(place, BF16))


def fell(z):
    near = z * (1.0 - z * (1.0 / 2 - z * (1.0 / 6 - z * (1.0 / 24 - z * (1.0 / 120 - z / 720)))))
    return jnp.where(z < 0.25, near, 1.0 - jnp.exp(-z))


def product(length, count, i, j):
    ratio = fell(1.0 / length) / jnp.sqrt(fell(2.0 / length))
    last = jnp.maximum(i, j)
    return ratio * jnp.exp(-jnp.abs(i - j) / length) * fell(2.0 * (count - last) / length)


def entered(length, count, i):
    ratio = fell(1.0 / length) / fell(2.0 / length)
    return ratio * jnp.exp(-(i + 1.0) / length) * fell(2.0 * (count - i) / length)


def tables_kernel(
    nx, share_ref, len_ref, wide_ref, e_ref, x_ref, v_ref, nh_ref, nl_ref, ab_ref, y_ref
):
    lev, ny, _ = nh_ref.shape
    length = wide_ref[...]
    fc, bc, d = jnp.sqrt(fell(2.0 / length)), fell(1.0 / length), jnp.exp(-1.0 / length)
    for k, value in enumerate(
        (d, fc, bc / fc, jnp.exp(-(nx + 1.0) / length), jnp.exp(1.0 / length), bc)
    ):
        e_ref[k] = value
    y_ref[0] = jnp.exp(-ny / length)
    y_ref[1] = entered(length, ny, 0.0)
    for i in range(3):
        y_ref[2 + i] = entered(length, ny, ny - 3.0 + i)
        y_ref[5 + i] = jnp.exp(-(3.0 - i) / length)
        y_ref[8 + i] = entered(length, ny, float(i))
        y_ref[11 + i] = jnp.exp(-(ny - float(i)) / length)

    row = lax.broadcasted_iota(jnp.int32, (8, ny), 0)
    at = row.astype(F32)
    top = row < 3
    for k in range(x_ref.shape[1]):
        own = jnp.full((8, ny), len_ref[share_ref[0] + k], F32)
        jump = jnp.exp(-nx / own)
        bottom = row > 4
        x_ref[0, k] = jnp.where(top, 0.0, jump)
        x_ref[1, k] = jnp.where(bottom, 0.0, jump)
        x_ref[2, k] = jnp.where(bottom, 0.0, entered(own, nx, 0.0))
        x_ref[3, k] = jnp.where(top, entered(own, nx, at), 0.0)
        x_ref[4, k] = jnp.where(top, jnp.exp(-(nx - at) / own), 0.0)
        x_ref[5, k] = jnp.where(bottom, entered(own, nx, nx - 8.0 + at), 0.0)
        x_ref[6, k] = jnp.where(bottom, jnp.exp(-(8.0 - at) / own), 0.0)

    cell = lax.broadcasted_iota(jnp.int32, (8, ny), 1)
    cells = cell.astype(F32)
    line = jnp.where(row < 4, at - 1.0, ny - 7.0 + at)
    zero = jnp.zeros((8, ny), F32)
    end, last = row < 3, row < 6
    lower = jnp.where(last & (cell == jnp.where(end, ny - 3 + row, row - 3)), 1.0, 0.0)
    place = jnp.concatenate([zero, lower], axis=0)
    across = lax.broadcasted_iota(jnp.int32, (ny, ny), 0).astype(F32)
    along = lax.broadcasted_iota(jnp.int32, (ny, ny), 1).astype(F32)
    apart, beyond = jnp.abs(across - along), ny - jnp.maximum(across, along)

    def level(l, carry):
        own = jnp.full((8, ny), len_ref[l], F32)
        root = jnp.sqrt(fell(2.0 / own))
        edge = jnp.where(
            row == 0, root * jnp.exp(-(ny - 1.0 - cells) / own), product(own, ny, line, cells)
        )
        high, low = split(jnp.where(row == 7, 0.0, edge))
        v_ref[l] = jnp.concatenate([high, low], axis=0)
        a, b = entered(own, ny, cells), jnp.exp(-(ny - cells) / own)
        part = jnp.where(end, a, b)
        high = part.astype(BF16).astype(F32)
        part = jnp.where((row == 2) | (row == 5), part - high, high)
        part = jnp.concatenate([jnp.where(last, part, 0.0), zero], axis=0)
        ab_ref[l] = jnp.concatenate([part, place], axis=1).astype(BF16)
        inverse = (1.0 / own)[:1]
        ratio = (fell(1.0 / own) / root)[:1]
        high, low = split(
            ratio * jnp.exp(-apart * inverse) * fell(2.0 * beyond * inverse)
        )
        nh_ref[l] = high
        nl_ref[l] = low
        return carry

    lax.fori_loop(0, lev, level, 0)


def body(
    increment,
    ensemble,
    wind_u,
    wind_v,
    filter_length,
    jacobian,
    obs_weight,
    departure,
    obs_home,
    obs_line,
    obs_count,
):
    count_x, count_y = lax.axis_size(GX), lax.axis_size(GY)
    homes = count_x * count_y
    pos_x, pos_y = lax.axis_index(GX), lax.axis_index(GY)
    lev, nx, ny = increment.shape
    members = ensemble.shape[0]
    channels = jacobian.shape[1]
    records = obs_home.shape[0]
    part = lev // CHUNKS
    share = part // count_x
    rows = (members + 1) * nx + 8
    deep = rows + 8

    named = (obs_home[:, None] == jnp.arange(homes, dtype=jnp.int32)[None, :]).astype(jnp.int32)
    table = jnp.stack(
        [
            jnp.sum(named * (obs_line[:, None] + 1), axis=0),
            jnp.sum(named * obs_count[:, None], axis=0),
        ]
    ).astype(BF16)
    meta = jnp.pad(table, ((1, 13), (0, 128 - homes)))
    jt = jnp.transpose(jacobian[0])
    b, mine = pl.pallas_call(
        sensor_kernel,
        out_shape=(
            jax.ShapeDtypeStruct((2 * lev, channels), BF16),
            jax.ShapeDtypeStruct((homes, lev // 2 + 16, 2 * lev), BF16),
        ),
        in_specs=[vmem()] * 3,
        out_specs=(vmem(), vmem()),
        compiler_params=params(8),
        name="sensor",
    )(jt, obs_weight, meta)
    gathered = lax.all_to_all(mine, BOTH, split_axis=0, concat_axis=0, tiled=True)

    per = min(8, records)
    qs = pl.pallas_call(
        records_kernel,
        grid_spec=pltpu.PrefetchScalarGridSpec(
            num_scalar_prefetch=2,
            grid=(records // per,),
            in_specs=[
                pl.BlockSpec((2 * lev, channels), lambda i, *_: (0, 0)),
                pl.BlockSpec((per, channels, ny), lambda i, *_: (i, 0, 0)),
            ],
            out_specs=[pl.BlockSpec((homes, part, ny), lambda i, *_: (0, 0, 0))] * CHUNKS,
        ),
        out_shape=[jax.ShapeDtypeStruct((homes, part, ny), BF16)] * CHUNKS,
        compiler_params=params(56),
        name="records",
    )(obs_home, obs_count, b, departure)
    qs, wind_u, wind_v = lax.optimization_barrier((qs, wind_u, wind_v))
    before, after = wind_ends(wind_u, wind_v)
    tables = pl.pallas_call(
        functools.partial(tables_kernel, nx),
        out_shape=(
            jax.ShapeDtypeStruct((6, lev, ny), F32),
            jax.ShapeDtypeStruct((7, share, 8, ny), F32),
            jax.ShapeDtypeStruct((lev, 16, ny), BF16),
            jax.ShapeDtypeStruct((lev, ny, ny), BF16),
            jax.ShapeDtypeStruct((lev, ny, ny), BF16),
            jax.ShapeDtypeStruct((lev, 16, 2 * ny), BF16),
            jax.ShapeDtypeStruct((14, lev, ny), F32),
        ),
        in_specs=[smem(), smem(), vmem()],
        out_specs=(vmem(),) * 7,
        compiler_params=params(12),
        name="tables",
    )(
        (pos_x * share).reshape(1),
        filter_length,
        jnp.broadcast_to(filter_length[:, None], (lev, ny)),
    )
    qs, before, after, tables = lax.optimization_barrier((qs, before, after, tables))
    arrived = [lax.all_to_all(q, BOTH, split_axis=0, concat_axis=0, tiled=True) for q in qs]

    seen = lax.dynamic_slice_in_dim(
        gathered[:, lev // 2 + 1 : lev // 2 + 3, :], pos_x * count_y + pos_y, 1, axis=2
    )[:, :, 0].astype(jnp.int32)
    asked, counts = seen[:, 0], seen[:, 1]
    g1 = pl.pallas_call(
        columns_kernel,
        out_shape=jax.ShapeDtypeStruct((lev * nx, ny), F32),
        in_specs=[smem(), smem(), vmem(), vmem()],
        out_specs=vmem(),
        scratch_shapes=[pltpu.VMEM((lev * nx, ny), F32)],
        compiler_params=params(12),
        cost_estimate=pl.CostEstimate(flops=2**33, bytes_accessed=2**23, transcendentals=0),
        name="columns",
    )(asked, counts, gathered, increment).reshape(lev, nx, ny)
    select = (asked[:, None] == jnp.arange(1, nx + 1, dtype=jnp.int32)[None, :]).astype(BF16)

    coef, table_x, edge, nh, nl, spread, coef_y = tables
    sides = wind_sides(wind_u, wind_v, before, after)
    g1, *sides = lax.optimization_barrier((g1, *sides))
    halo_u, halo_v = padded_winds(wind_u, wind_v, (before, after, *sides))
    arrived, halo_u, halo_v, g1 = lax.optimization_barrier((arrived, halo_u, halo_v, g1))

    alpha = static = None
    for c in range(CHUNKS):
        g2 = jnp.einsum("sx,sly->lxy", select, arrived[c], preferred_element_type=F32)
        steps = part // 16
        off = c * steps
        h = pl.pallas_call(
            edges_kernel,
            grid=(steps,),
            in_specs=[
                pl.BlockSpec((16, nx, ny), lambda i, off=off: (off + i, 0, 0)),
                pl.BlockSpec((16, nx, ny), lambda i: (i, 0, 0)),
                pl.BlockSpec((members, 16, nx, ny), lambda i, off=off: (0, off + i, 0, 0)),
                pl.BlockSpec((6, 16, ny), lambda i, off=off: (0, off + i, 0)),
            ],
            out_specs=pl.BlockSpec((16, 16, ny), lambda i: (i, 0, 0)),
            out_shape=jax.ShapeDtypeStruct((part, 16, ny), BF16),
            scratch_shapes=[pltpu.VMEM((16 * rows, ny), F32), pltpu.VMEM((16 * 16, ny), F32)],
            compiler_params=params(56),
            name=f"edges_{c}",
        )(g1, g2, ensemble, coef)
        h = lax.all_to_all(
            h.reshape(count_x, share, 16, ny), GX, split_axis=0, concat_axis=0, tiled=True
        )
        h = pl.pallas_call(
            scan_x_kernel,
            out_shape=jax.ShapeDtypeStruct(h.shape, BF16),
            in_specs=[vmem(), vmem()],
            out_specs=vmem(),
            compiler_params=params(8),
            name=f"scan_x_{c}",
        )(h, table_x)
        h = lax.all_to_all(h, GX, split_axis=0, concat_axis=0, tiled=True).reshape(part, 16, ny)
        hi, lo, es, to_right, to_left = pl.pallas_call(
            filter_x_kernel,
            grid=(steps,),
            in_specs=[
                pl.BlockSpec((16, nx, ny), lambda i, off=off: (off + i, 0, 0)),
                pl.BlockSpec((16, nx, ny), lambda i: (i, 0, 0)),
                pl.BlockSpec((members, 16, nx, ny), lambda i, off=off: (0, off + i, 0, 0)),
                pl.BlockSpec((16, 16, ny), lambda i: (i, 0, 0)),
                pl.BlockSpec((6, 16, ny), lambda i, off=off: (0, off + i, 0)),
                pl.BlockSpec((16, 16, ny), lambda i, off=off: (off + i, 0, 0)),
            ],
            out_specs=(
                pl.BlockSpec((16, deep, ny), lambda i: (i, 0, 0)),
                pl.BlockSpec((16, deep, ny), lambda i: (i, 0, 0)),
                pl.BlockSpec((count_y, 2, 16, deep), lambda i: (0, 0, i, 0)),
                pl.BlockSpec((3, 16, ny), lambda i: (0, i, 0)),
                pl.BlockSpec((3, 16, ny), lambda i: (0, i, 0)),
            ),
            out_shape=(
                jax.ShapeDtypeStruct((part, deep, ny), BF16),
                jax.ShapeDtypeStruct((part, deep, ny), BF16),
                jax.ShapeDtypeStruct((count_y, 2, part, deep), BF16),
                jax.ShapeDtypeStruct((3, part, ny), BF16),
                jax.ShapeDtypeStruct((3, part, ny), BF16),
            ),
            scratch_shapes=[
                pltpu.VMEM((16 * rows, ny), F32),
                pltpu.VMEM((16 * (deep + 8), ny), F32),
                pltpu.VMEM((16 * 16, ny), F32),
                pltpu.VMEM((16 * 16, ny), F32),
            ],
            compiler_params=params(56),
            name=f"filter_x_{c}",
        )(g1, g2, ensemble, h, coef, edge)
        es = lax.all_to_all(es, GY, split_axis=0, concat_axis=0, tiled=True)
        from_left = from_before(to_right, GY)
        from_right = from_after(to_left, GY)
        fb = pl.pallas_call(
            scan_y_kernel,
            out_shape=jax.ShapeDtypeStruct((part * 16, deep), BF16),
            in_specs=[smem()] + [vmem()] * 4,
            out_specs=vmem(),
            scratch_shapes=[
                pltpu.VMEM((count_y, part, deep), F32),
                pltpu.VMEM((count_y, part, deep), F32),
                pltpu.VMEM((2, part * 16, deep // 2), F32),
            ],
            compiler_params=params(16),
            name=f"scan_y_{c}",
        )(pos_y.reshape(1), es, from_left, from_right, coef_y[:, c * part : (c + 1) * part])
        steps = part // 8
        off = c * steps
        extra = () if c == 0 else (alpha, static)
        alpha, static = pl.pallas_call(
            final_kernel,
            grid=(steps,),
            in_specs=[
                pl.BlockSpec((8, deep, ny), lambda i: (i, 0, 0)),
                pl.BlockSpec((8, deep, ny), lambda i: (i, 0, 0)),
                pl.BlockSpec((8, ny, ny), lambda i, off=off: (off + i, 0, 0)),
                pl.BlockSpec((8, ny, ny), lambda i, off=off: (off + i, 0, 0)),
                pl.BlockSpec((8 * 16, deep), lambda i: (i, 0)),
                pl.BlockSpec((8, 16, 2 * ny), lambda i, off=off: (off + i, 0, 0)),
                pl.BlockSpec((8, nx + 8, 2 * ny), lambda i, off=off: (off + i, 0, 0)),
                pl.BlockSpec((8, nx + 8, 2 * ny), lambda i, off=off: (off + i, 0, 0)),
            ]
            + [pl.BlockSpec(memory_space=pl.ANY)] * len(extra),
            out_specs=(
                pl.BlockSpec((members, 8, nx, ny), lambda i, off=off: (0, off + i, 0, 0)),
                pl.BlockSpec((8, nx, ny), lambda i, off=off: (off + i, 0, 0)),
            ),
            out_shape=(
                jax.ShapeDtypeStruct((members, lev, nx, ny), F32),
                jax.ShapeDtypeStruct((lev, nx, ny), F32),
            ),
            input_output_aliases={8: 0, 9: 1} if extra else {},
            compiler_params=params(56),
            name=f"final_{c}",
        )(hi, lo, nh, nl, fb, spread, halo_u, halo_v, *extra)
    return alpha, static


def solution(mesh):
    grid = P(None, GX, GY)
    placed = (
        grid,
        P(None, None, GX, GY),
        grid,
        grid,
        P(),
        P(BOTH, None, None),
        P(BOTH, None),
        P(BOTH, None, None),
        P(BOTH),
        P(BOTH),
        P(BOTH),
    )
    return jax.shard_map(
        body,
        mesh=mesh,
        in_specs=placed,
        out_specs=(P(None, None, GX, GY), grid),
        check_vma=False,
    )
```

```python
import functools

import jax
import jax.numpy as jnp
import numpy as np
from jax import lax
from jax.experimental import pallas as pl
from jax.experimental.pallas import tpu as pltpu
from jax.sharding import PartitionSpec as P

GX, GY = "gx", "gy"
BOTH = (GX, GY)
CHUNKS = 1
MIB = 2**20
F32, BF16 = jnp.float32, jnp.bfloat16

NT = (((1,), (1,)), ((), ()))
TN = (((0,), (0,)), ((), ()))


def vmem():
    return pl.BlockSpec(memory_space=pltpu.VMEM)


def smem():
    return pl.BlockSpec(memory_space=pltpu.SMEM)


def params(mib):
    return pltpu.CompilerParams(vmem_limit_bytes=mib * MIB)


def split(value):
    high = value.astype(BF16)
    return high, (value - high.astype(F32)).astype(BF16)


def sensor_kernel(jt_ref, w_ref, meta_ref, b_ref, out_ref):
    lev = jt_ref.shape[0]
    high, low = split(jt_ref[...].astype(F32) * w_ref[...])
    b_ref[:lev] = high
    b_ref[lev:] = low
    a = lax.dot_general(high, jt_ref[...], NT, preferred_element_type=F32)
    a += lax.dot_general(low, jt_ref[...], NT, preferred_element_type=F32)
    row = lax.broadcasted_iota(jnp.int32, a.shape, 0)
    col = lax.broadcasted_iota(jnp.int32, a.shape, 1)
    high = a.astype(BF16).astype(F32)
    packed = jnp.where(col >= row, high, a - high)
    diagonal = jnp.sum(jnp.where(col == row, a - high, 0.0), axis=0, keepdims=True)
    half = lev // 2
    packed = jnp.concatenate([packed[:half], packed[half:]], axis=1)
    meta = meta_ref[...].astype(F32)
    first = lax.broadcasted_iota(jnp.int32, meta.shape, 0) == 0
    meta = jnp.where(first, jnp.concatenate([diagonal, jnp.zeros_like(diagonal)], axis=1), meta)
    whole = jnp.concatenate([packed, meta], axis=0).astype(BF16)

    def copy(k, carry):
        out_ref[k] = whole
        return carry

    lax.fori_loop(0, out_ref.shape[0], copy, 0, unroll=8)


def records_kernel(home_ref, count_ref, b_ref, dep_ref, *outs):
    step, per = pl.program_id(0), dep_ref.shape[0]
    lev = b_ref.shape[0] // 2
    part = lev // len(outs)

    @pl.when(step == 0)
    def _():
        for out in outs:
            out[...] = jnp.zeros_like(out)

    lane = lax.broadcasted_iota(jnp.int32, (lev, dep_ref.shape[2]), 1)
    for k in range(per):
        both = jnp.dot(b_ref[...], dep_ref[k], preferred_element_type=F32)
        q = both[:lev] + both[lev:]
        q = jnp.where(lane < count_ref[step * per + k], q, 0.0).astype(BF16)
        for c, out in enumerate(outs):
            out[home_ref[step * per + k]] = q[c * part : (c + 1) * part]


def columns_kernel(line_ref, count_ref, gathered_ref, inc_ref, g_ref, x_ref):
    lev, nx, ny = inc_ref.shape
    for l in range(lev):
        x_ref[pl.ds(l * nx, nx), :] = inc_ref[l].astype(F32)
    g_ref[...] = jnp.zeros_like(g_ref)
    lane = lax.broadcasted_iota(jnp.int32, (lev, ny), 1)
    half = lev // 2
    eye = lax.broadcasted_iota(jnp.int32, (lev, lev), 0) == lax.broadcasted_iota(
        jnp.int32, (lev, lev), 1
    )
    group = 4

    def some(i, carry):
        found = []
        for k in range(group):
            s = i * group + k
            at = jnp.maximum(line_ref[s] - 1, 0)
            x = x_ref[pl.ds(at, lev, stride=nx), :].astype(BF16)
            kept = gathered_ref[s, :half].astype(F32)
            m = jnp.concatenate([kept[:, :lev], kept[:, lev:]], axis=0)
            diagonal = gathered_ref[s, half : half + 16].astype(F32)[:1, :lev]
            other = jnp.where(eye, diagonal, jnp.transpose(m))
            y = jnp.dot(
                jnp.concatenate([m, other], axis=1).astype(BF16),
                jnp.concatenate([x, x], axis=0),
                preferred_element_type=F32,
            )
            found.append((at, jnp.where(lane < count_ref[s], y, 0.0)))
        for at, y in found:
            g_ref[pl.ds(at, lev, stride=nx), :] += y
        return carry

    lax.fori_loop(0, line_ref.shape[0] // group, some, 0)


def lay_fields(g1_ref, g2_ref, ens_ref, f_ref):
    members, block, nx, ny = ens_ref.shape
    rows = (members + 1) * nx + 8
    for l in range(block):
        g = g1_ref[l] - g2_ref[l]
        f_ref[pl.ds(l * rows + members * nx, nx), :] = g
        for m in range(members):
            f_ref[pl.ds(l * rows + m * nx, nx), :] = ens_ref[m, l].astype(F32) * g


def edges_kernel(g1_ref, g2_ref, ens_ref, coef_ref, h_ref, f_ref, tmp_ref):
    members, block, nx, ny = ens_ref.shape
    fields = members + 1
    rows = fields * nx + 8
    lay_fields(g1_ref, g2_ref, ens_ref, f_ref)

    for base in range(0, block, 8):
        d, fc, rt, d49, inv = (coef_ref[k, base : base + 8] for k in range(5))

        def line(m, x, base=base):
            return f_ref[pl.ds(base * rows + m * nx + x, 8, stride=rows), :]

        ahead = [line(m, 0) for m in range(fields)]
        back = [line(m, nx - 1) for m in range(fields)]
        for x in range(1, nx):
            for m in range(fields):
                ahead[m] = d * ahead[m] + line(m, x)
                back[m] = d * back[m] + line(m, nx - 1 - x)

        def put(row, value, base=base):
            tmp_ref[pl.ds(base * 16 + row, 8, stride=16), :] = value

        for m in range(fields):
            put(3 + m, fc * ahead[m])
            put(8 + m, rt * (back[m] - d49 * ahead[m]))
        e, p = ahead[members], back[members]
        f0, f1 = line(members, 0), line(members, 1)
        f46, f47 = line(members, nx - 2), line(members, nx - 1)
        d48, d47 = d49 * inv, d49 * inv * inv
        p1 = (p - f0) * inv
        p2 = (p1 - f1) * inv
        put(0, rt * (p - d49 * e))
        put(1, rt * (d * f0 + p1 - d48 * e))
        put(2, rt * (d * (d * f0 + f1) + p2 - d47 * e))
        e1 = (e - f47) * inv
        e2 = (e1 - f46) * inv
        put(13, rt * (e2 + d * (f46 + d * f47) - d * d * d * d * e))
        put(14, rt * (e1 + d * f47 - d * d * d * e))
        put(15, rt * (e - d * d * e))
    for l in range(block):
        h_ref[l] = tmp_ref[pl.ds(l * 16, 16), :].astype(BF16)


def scan_x_kernel(in_ref, coef_ref, out_ref):
    count, levels = in_ref.shape[:2]
    row = lax.broadcasted_iota(jnp.int32, (8, in_ref.shape[3]), 0)
    for l in range(levels):
        d0, d1, kappa, a0, b0, a1, b1 = (coef_ref[k, l] for k in range(7))
        first, second = [], []
        for g in range(count):
            v = in_ref[g, l].astype(F32)
            first.append(v[:8])
            second.append(v[8:])
        ahead = [jnp.zeros_like(row, F32)]
        for g in range(count - 1):
            ahead.append(first[g] + d0 * ahead[g])
        turned = [pltpu.roll(a, 5, 0) for a in ahead]
        back = [jnp.zeros_like(row, F32)] * count
        for g in range(count - 1, 0, -1):
            back[g - 1] = second[g] + kappa * turned[g] + d1 * back[g]
        static = [(ahead[g][7:8], back[g][4:5]) for g in range(count)]
        low = [first[g] + a0 * static[g][0] + b0 * static[g][1] for g in range(count)]
        high = [second[g] + a1 * static[g][0] + b1 * static[g][1] for g in range(count)]
        none = jnp.zeros_like(row, F32)
        for g in range(count):
            after = low[g + 1] if g + 1 < count else none
            before = high[g - 1] if g > 0 else none
            out_ref[g, l] = jnp.concatenate(
                [jnp.where(row < 3, after, ahead[g]), jnp.where(row < 5, back[g], before)], axis=0
            ).astype(BF16)


def filter_x_kernel(
    g1_ref,
    g2_ref,
    ens_ref,
    fb_ref,
    coef_ref,
    v_ref,
    hi_ref,
    lo_ref,
    es_ref,
    right_ref,
    left_ref,
    f_ref,
    xs_ref,
    st_ref,
    ey_ref,
):
    members, block, nx, _ = ens_ref.shape
    fields = members + 1
    used = fields * nx
    rows = used + 8
    lay_fields(g1_ref, g2_ref, ens_ref, f_ref)
    deep = hi_ref.shape[1]
    wide = deep + 8
    for l in range(block):
        st_ref[pl.ds(l * 16, 16), :] = fb_ref[l].astype(F32)
    for base in range(0, block, 8):
        d, fc, bc = (coef_ref[k, base : base + 8] for k in (0, 1, 5))

        def at(m, x, base=base):
            return pl.ds(base * wide + m * nx + x, 8, stride=wide)

        state = [st_ref[pl.ds(base * 16 + 3 + m, 8, stride=16), :] for m in range(fields)]
        for x in range(nx):
            for m in range(fields):
                f = f_ref[pl.ds(base * rows + m * nx + x, 8, stride=rows), :]
                state[m] = fc * f + d * state[m]
                xs_ref[at(m, x), :] = state[m]
        state = [st_ref[pl.ds(base * 16 + 8 + m, 8, stride=16), :] for m in range(fields)]
        for x in range(nx - 1, -1, -1):
            for m in range(fields):
                state[m] = bc * xs_ref[at(m, x), :] + d * state[m]
                xs_ref[at(m, x), :] = state[m]
    row = lax.broadcasted_iota(jnp.int32, (8, f_ref.shape[1]), 0)
    for l in range(block):
        after, before = st_ref[pl.ds(l * 16, 8), :], st_ref[pl.ds(l * 16 + 8, 8), :]
        halo = jnp.where(row < 3, after, jnp.where(row < 5, 0.0, before))
        xs_ref[pl.ds(l * wide + used, 8), :] = halo
        xs_ref[pl.ds(l * wide + used + 8, 8), :] = jnp.zeros_like(halo)
        hi, lo = split(xs_ref[pl.ds(l * wide, deep), :])
        hi_ref[l] = hi
        lo_ref[l] = lo
        one = lax.dot_general(v_ref[l], hi, NT, preferred_element_type=F32)
        two = lax.dot_general(v_ref[l], lo, NT, preferred_element_type=F32)
        ey_ref[pl.ds(l, 8, stride=block), :] = (one[:8] + one[8:] + two[:8])[:, : deep // 2]
        ey_ref[pl.ds(8 * block + l, 8, stride=block), :] = (one[:8] + one[8:] + two[:8])[
            :, deep // 2 :
        ]

    def both(q, side):
        return ey_ref[pl.ds((8 * side + q) * block, block), :].astype(BF16)

    for q in range(2):
        for side in range(2):
            got = both(q, side)
            lanes = pl.ds(side * got.shape[1], got.shape[1])
            for k in range(es_ref.shape[0]):
                es_ref[k, q, :, lanes] = got
    for q in range(3):
        left_ref[q] = both(1 + q, 1)
        right_ref[q] = both(4 + q, 1)


def scan_y_kernel(me_ref, es_ref, fl_ref, fr_ref, coef_ref, out_ref, ahead_ref, back_ref, tmp_ref):
    count, _, lev, lanes = es_ref.shape
    half = lanes // 2
    me = me_ref[0]
    decay, kappa = coef_ref[0], coef_ref[1]
    for side in range(2):
        part = pl.ds(side * half, half)
        state = jnp.zeros((lev, half), F32)
        ahead_ref[0, :, part] = state
        for k in range(count - 1):
            state = es_ref[k, 0, :, part].astype(F32) + decay * state
            ahead_ref[k + 1, :, part] = state
        state = jnp.zeros((lev, half), F32)
        back_ref[count - 1, :, part] = state
        for k in range(count - 1, 0, -1):
            state = (
                es_ref[k, 1, :, part].astype(F32)
                + kappa * ahead_ref[k, :, part]
                + decay * state
            )
            back_ref[k - 1, :, part] = state
    none = jnp.zeros((lev, half), F32)

    def put(q, side, value):
        tmp_ref[side, pl.ds(q, lev, stride=16), :] = value

    for side in range(2):
        part = pl.ds(side * half, half)
        for first, ref in ((0, ahead_ref), (3, back_ref)):
            value = ref[me, :, part]
            high = value.astype(BF16).astype(F32)
            put(first, side, high)
            put(first + 1, side, value - high)
            put(first + 2, side, high)
        for q in (6, 7, 14, 15):
            put(q, side, none)
    before, after = jnp.maximum(me - 1, 0), jnp.minimum(me + 1, count - 1)
    part = pl.ds(half, half)
    for q in range(3):
        put(8 + q, 0, none)
        put(11 + q, 0, none)
        value = (
            fl_ref[q].astype(F32)
            + coef_ref[2 + q] * ahead_ref[before, :, part]
            + coef_ref[5 + q] * back_ref[before, :, part]
        )
        put(8 + q, 1, jnp.where(me > 0, value, 0.0))
        value = (
            fr_ref[q].astype(F32)
            + coef_ref[8 + q] * ahead_ref[after, :, part]
            + coef_ref[11 + q] * back_ref[after, :, part]
        )
        put(11 + q, 1, jnp.where(me < count - 1, value, 0.0))
    for side in range(2):
        out_ref[:, pl.ds(side * half, half)] = tmp_ref[side].astype(BF16)


def final_kernel(hi_ref, lo_ref, nh_ref, nl_ref, fb_ref, ab_ref, u_ref, v_ref, *rest):
    alpha_ref, static_ref = rest[-2:]
    block = hi_ref.shape[0]
    members, _, nx, ny = alpha_ref.shape
    first = members * nx
    deep = nx + 8
    wide = 2 * ny
    for l in range(block):
        hi = hi_ref[l]
        more = lax.dot_general(
            fb_ref[pl.ds(l * 16, 16), :], ab_ref[l], TN, preferred_element_type=F32
        )
        got = jnp.dot(hi, nh_ref[l], preferred_element_type=F32)
        got += jnp.dot(hi, nl_ref[l], preferred_element_type=F32)
        got += jnp.dot(lo_ref[l], nh_ref[l], preferred_element_type=F32)
        got += more[:, :ny]
        for m in range(members):
            alpha_ref[m, l] = got[m * nx : (m + 1) * nx]
        s = jnp.concatenate(
            [got[first : first + deep], more[first : first + deep, ny:]], axis=1
        )
        u, v = u_ref[l].astype(F32), v_ref[l].astype(F32)
        up, vp = u > 0.0, v > 0.0
        u, v = jnp.abs(u), jnp.abs(v)
        for _ in range(3):
            s = s + u * (jnp.where(up, pltpu.roll(s, 1, 0), pltpu.roll(s, deep - 1, 0)) - s)
            s = s + v * (jnp.where(vp, pltpu.roll(s, 1, 1), pltpu.roll(s, wide - 1, 1)) - s)
        static_ref[l] = s[:nx, :ny]


def from_before(array, axis):
    count = lax.axis_size(axis)
    return lax.ppermute(array, axis, [(i, i + 1) for i in range(count - 1)])


def from_after(array, axis):
    count = lax.axis_size(axis)
    return lax.ppermute(array, axis, [(i + 1, i) for i in range(count - 1)])


def wind_rows_kernel(u_ref, v_ref, first_ref, last_ref):
    nx = u_ref.shape[1]
    for l in range(u_ref.shape[0]):
        u, v = u_ref[l].astype(F32), v_ref[l].astype(F32)
        first_ref[l] = jnp.concatenate([u[:8], v[:8]], axis=0).astype(BF16)
        last_ref[l] = jnp.concatenate([u[nx - 8 :], v[nx - 8 :]], axis=0).astype(BF16)


def taller(u_ref, v_ref, before_ref, after_ref, l):
    before, after = before_ref[l].astype(F32), after_ref[l].astype(F32)
    row = lax.broadcasted_iota(jnp.int32, (8, before.shape[1]), 0)
    both = []
    for k, ref in enumerate((u_ref, v_ref)):
        part = slice(8 * k, 8 * k + 8)
        halo = jnp.where(row < 3, after[part], jnp.where(row > 4, before[part], 0.0))
        both.append(jnp.concatenate([ref[l].astype(F32), halo], axis=0))
    return both


def wind_columns_kernel(u_ref, v_ref, before_ref, after_ref, pick_ref, right_ref, left_ref):
    for l in range(u_ref.shape[0]):
        u, v = taller(u_ref, v_ref, before_ref, after_ref, l)
        gap = jnp.zeros((8, u.shape[1]), F32)
        both = jnp.concatenate([u, gap, v, gap], axis=0).astype(BF16)
        got = lax.dot_general(pick_ref[...], both, NT, preferred_element_type=F32)
        half = got.shape[1] // 2
        for k, ref in enumerate((right_ref, left_ref)):
            some = got[8 * k : 8 * k + 8]
            ref[l] = jnp.concatenate([some[:, :half], some[:, half:]], axis=0).astype(BF16)


def wind_pad_kernel(
    u_ref, v_ref, before_ref, after_ref, left_ref, right_ref, place_ref, out_u_ref, out_v_ref
):
    ny = u_ref.shape[2]
    for l in range(u_ref.shape[0]):
        u, v = taller(u_ref, v_ref, before_ref, after_ref, l)
        sides = jnp.concatenate([left_ref[l], right_ref[l]], axis=0)
        got = lax.dot_general(sides, place_ref[...], TN, preferred_element_type=F32)[: len(u)]
        out_u_ref[l] = jnp.concatenate([u, got[:, :ny]], axis=1).astype(BF16)
        out_v_ref[l] = jnp.concatenate([v, got[:, ny:]], axis=1).astype(BF16)


def levels(*shape):
    return pl.BlockSpec((16, *shape), lambda i: (i, *(0 for _ in shape)))


def whole(*shape):
    return pl.BlockSpec(shape, lambda i: tuple(0 for _ in shape))


def wind_ends(wind_u, wind_v):
    lev, nx, ny = wind_u.shape
    steps = (lev // 16,)
    first, last = pl.pallas_call(
        wind_rows_kernel,
        grid=steps,
        in_specs=[levels(nx, ny)] * 2,
        out_specs=(levels(16, ny),) * 2,
        out_shape=(jax.ShapeDtypeStruct((lev, 16, ny), BF16),) * 2,
        compiler_params=params(8),
        name="wind_rows",
    )(wind_u, wind_v)
    return from_before(last, GX), from_after(first, GX)


def wind_sides(wind_u, wind_v, before, after):
    lev, nx, ny = wind_u.shape
    deep = nx + 16
    steps = (lev // 16,)
    pick = np.zeros((16, ny), np.float32)
    for k in range(3):
        pick[k, ny - 3 + k] = pick[8 + k, k] = 1
    right, left = pl.pallas_call(
        wind_columns_kernel,
        grid=steps,
        in_specs=[levels(nx, ny)] * 2 + [levels(16, ny)] * 2 + [whole(16, ny)],
        out_specs=(levels(16, deep),) * 2,
        out_shape=(jax.ShapeDtypeStruct((lev, 16, deep), BF16),) * 2,
        compiler_params=params(8),
        name="wind_columns",
    )(wind_u, wind_v, before, after, jnp.asarray(pick, BF16))
    return from_before(right, GY), from_after(left, GY)


def padded_winds(wind_u, wind_v, halos):
    lev, nx, ny = wind_u.shape
    deep = nx + 16
    place = np.zeros((32, 2 * ny), np.float32)
    for k in range(3):
        place[k, ny - 3 + k] = place[16 + k, k] = 1
        place[8 + k, 2 * ny - 3 + k] = place[24 + k, ny + k] = 1
    return pl.pallas_call(
        wind_pad_kernel,
        grid=(lev // 16,),
        in_specs=[levels(nx, ny)] * 2
        + [levels(16, ny)] * 2
        + [levels(16, deep)] * 2
        + [whole(32, 2 * ny)],
        out_specs=(levels(nx + 8, 2 * ny),) * 2,
        out_shape=(jax.ShapeDtypeStruct((lev, nx + 8, 2 * ny), BF16),) * 2,
        compiler_params=params(8),
        name="wind_pad",
    )(wind_u, wind_v, *halos, jnp.asarray(place, BF16))


def fell(z):
    near = z * (1.0 - z * (1.0 / 2 - z * (1.0 / 6 - z * (1.0 / 24 - z * (1.0 / 120 - z / 720)))))
    return jnp.where(z < 0.25, near, 1.0 - jnp.exp(-z))


def product(length, count, i, j):
    ratio = fell(1.0 / length) / jnp.sqrt(fell(2.0 / length))
    last = jnp.maximum(i, j)
    return ratio * jnp.exp(-jnp.abs(i - j) / length) * fell(2.0 * (count - last) / length)


def entered(length, count, i):
    ratio = fell(1.0 / length) / fell(2.0 / length)
    return ratio * jnp.exp(-(i + 1.0) / length) * fell(2.0 * (count - i) / length)


def tables_kernel(
    nx, share_ref, len_ref, wide_ref, e_ref, x_ref, v_ref, nh_ref, nl_ref, ab_ref, y_ref
):
    lev, ny, _ = nh_ref.shape
    length = wide_ref[...]
    fc, bc, d = jnp.sqrt(fell(2.0 / length)), fell(1.0 / length), jnp.exp(-1.0 / length)
    for k, value in enumerate(
        (d, fc, bc / fc, jnp.exp(-(nx + 1.0) / length), jnp.exp(1.0 / length), bc)
    ):
        e_ref[k] = value
    y_ref[0] = jnp.exp(-ny / length)
    y_ref[1] = entered(length, ny, 0.0)
    for i in range(3):
        y_ref[2 + i] = entered(length, ny, ny - 3.0 + i)
        y_ref[5 + i] = jnp.exp(-(3.0 - i) / length)
        y_ref[8 + i] = entered(length, ny, float(i))
        y_ref[11 + i] = jnp.exp(-(ny - float(i)) / length)

    row = lax.broadcasted_iota(jnp.int32, (8, ny), 0)
    at = row.astype(F32)
    top = row < 3
    for k in range(x_ref.shape[1]):
        own = jnp.full((8, ny), len_ref[share_ref[0] + k], F32)
        jump = jnp.exp(-nx / own)
        bottom = row > 4
        x_ref[0, k] = jnp.where(top, 0.0, jump)
        x_ref[1, k] = jnp.where(bottom, 0.0, jump)
        x_ref[2, k] = jnp.where(bottom, 0.0, entered(own, nx, 0.0))
        x_ref[3, k] = jnp.where(top, entered(own, nx, at), 0.0)
        x_ref[4, k] = jnp.where(top, jnp.exp(-(nx - at) / own), 0.0)
        x_ref[5, k] = jnp.where(bottom, entered(own, nx, nx - 8.0 + at), 0.0)
        x_ref[6, k] = jnp.where(bottom, jnp.exp(-(8.0 - at) / own), 0.0)

    cell = lax.broadcasted_iota(jnp.int32, (8, ny), 1)
    cells = cell.astype(F32)
    line = jnp.where(row < 4, at - 1.0, ny - 7.0 + at)
    zero = jnp.zeros((8, ny), F32)
    end, last = row < 3, row < 6
    lower = jnp.where(last & (cell == jnp.where(end, ny - 3 + row, row - 3)), 1.0, 0.0)
    place = jnp.concatenate([zero, lower], axis=0)
    across = lax.broadcasted_iota(jnp.int32, (ny, ny), 0).astype(F32)
    along = lax.broadcasted_iota(jnp.int32, (ny, ny), 1).astype(F32)
    apart, beyond = jnp.abs(across - along), ny - jnp.maximum(across, along)

    def level(l, carry):
        own = jnp.full((8, ny), len_ref[l], F32)
        root = jnp.sqrt(fell(2.0 / own))
        edge = jnp.where(
            row == 0, root * jnp.exp(-(ny - 1.0 - cells) / own), product(own, ny, line, cells)
        )
        high, low = split(jnp.where(row == 7, 0.0, edge))
        v_ref[l] = jnp.concatenate([high, low], axis=0)
        a, b = entered(own, ny, cells), jnp.exp(-(ny - cells) / own)
        part = jnp.where(end, a, b)
        high = part.astype(BF16).astype(F32)
        part = jnp.where((row == 2) | (row == 5), part - high, high)
        part = jnp.concatenate([jnp.where(last, part, 0.0), zero], axis=0)
        ab_ref[l] = jnp.concatenate([part, place], axis=1).astype(BF16)
        inverse = (1.0 / own)[:1]
        ratio = (fell(1.0 / own) / root)[:1]
        high, low = split(
            ratio * jnp.exp(-apart * inverse) * fell(2.0 * beyond * inverse)
        )
        nh_ref[l] = high
        nl_ref[l] = low
        return carry

    lax.fori_loop(0, lev, level, 0)


def body(
    increment,
    ensemble,
    wind_u,
    wind_v,
    filter_length,
    jacobian,
    obs_weight,
    departure,
    obs_home,
    obs_line,
    obs_count,
):
    count_x, count_y = lax.axis_size(GX), lax.axis_size(GY)
    homes = count_x * count_y
    pos_x, pos_y = lax.axis_index(GX), lax.axis_index(GY)
    lev, nx, ny = increment.shape
    members = ensemble.shape[0]
    channels = jacobian.shape[1]
    records = obs_home.shape[0]
    part = lev // CHUNKS
    share = part // count_x
    rows = (members + 1) * nx + 8
    deep = rows + 8

    named = (obs_home[:, None] == jnp.arange(homes, dtype=jnp.int32)[None, :]).astype(jnp.int32)
    table = jnp.stack(
        [
            jnp.sum(named * (obs_line[:, None] + 1), axis=0),
            jnp.sum(named * obs_count[:, None], axis=0),
        ]
    ).astype(BF16)
    meta = jnp.pad(table, ((1, 13), (0, 128 - homes)))
    jt = jnp.transpose(jacobian[0])
    b, mine = pl.pallas_call(
        sensor_kernel,
        out_shape=(
            jax.ShapeDtypeStruct((2 * lev, channels), BF16),
            jax.ShapeDtypeStruct((homes, lev // 2 + 16, 2 * lev), BF16),
        ),
        in_specs=[vmem()] * 3,
        out_specs=(vmem(), vmem()),
        compiler_params=params(8),
        name="sensor",
    )(jt, obs_weight, meta)
    gathered = lax.all_to_all(mine, BOTH, split_axis=0, concat_axis=0, tiled=True)

    per = min(8, records)
    qs = pl.pallas_call(
        records_kernel,
        grid_spec=pltpu.PrefetchScalarGridSpec(
            num_scalar_prefetch=2,
            grid=(records // per,),
            in_specs=[
                pl.BlockSpec((2 * lev, channels), lambda i, *_: (0, 0)),
                pl.BlockSpec((per, channels, ny), lambda i, *_: (i, 0, 0)),
            ],
            out_specs=[pl.BlockSpec((homes, part, ny), lambda i, *_: (0, 0, 0))] * CHUNKS,
        ),
        out_shape=[jax.ShapeDtypeStruct((homes, part, ny), BF16)] * CHUNKS,
        compiler_params=params(56),
        name="records",
    )(obs_home, obs_count, b, departure)
    qs, wind_u, wind_v = lax.optimization_barrier((qs, wind_u, wind_v))
    before, after = wind_ends(wind_u, wind_v)
    tables = pl.pallas_call(
        functools.partial(tables_kernel, nx),
        out_shape=(
            jax.ShapeDtypeStruct((6, lev, ny), F32),
            jax.ShapeDtypeStruct((7, share, 8, ny), F32),
            jax.ShapeDtypeStruct((lev, 16, ny), BF16),
            jax.ShapeDtypeStruct((lev, ny, ny), BF16),
            jax.ShapeDtypeStruct((lev, ny, ny), BF16),
            jax.ShapeDtypeStruct((lev, 16, 2 * ny), BF16),
            jax.ShapeDtypeStruct((14, lev, ny), F32),
        ),
        in_specs=[smem(), smem(), vmem()],
        out_specs=(vmem(),) * 7,
        compiler_params=params(12),
        name="tables",
    )(
        (pos_x * share).reshape(1),
        filter_length,
        jnp.broadcast_to(filter_length[:, None], (lev, ny)),
    )
    qs, before, after, tables = lax.optimization_barrier((qs, before, after, tables))
    arrived = [lax.all_to_all(q, BOTH, split_axis=0, concat_axis=0, tiled=True) for q in qs]

    seen = lax.dynamic_slice_in_dim(
        gathered[:, lev // 2 + 1 : lev // 2 + 3, :], pos_x * count_y + pos_y, 1, axis=2
    )[:, :, 0].astype(jnp.int32)
    asked, counts = seen[:, 0], seen[:, 1]
    g1 = pl.pallas_call(
        columns_kernel,
        out_shape=jax.ShapeDtypeStruct((lev * nx, ny), F32),
        in_specs=[smem(), smem(), vmem(), vmem()],
        out_specs=vmem(),
        scratch_shapes=[pltpu.VMEM((lev * nx, ny), F32)],
        compiler_params=params(12),
        cost_estimate=pl.CostEstimate(flops=2**33, bytes_accessed=2**23, transcendentals=0),
        name="columns",
    )(asked, counts, gathered, increment).reshape(lev, nx, ny)
    select = (asked[:, None] == jnp.arange(1, nx + 1, dtype=jnp.int32)[None, :]).astype(BF16)

    coef, table_x, edge, nh, nl, spread, coef_y = tables
    sides = wind_sides(wind_u, wind_v, before, after)
    arrived, g1 = lax.optimization_barrier((arrived, g1))

    alpha = static = None
    for c in range(CHUNKS):
        g2 = jnp.einsum("sx,sly->lxy", select, arrived[c], preferred_element_type=F32)
        steps = part // 16
        off = c * steps
        h = pl.pallas_call(
            edges_kernel,
            grid=(steps,),
            in_specs=[
                pl.BlockSpec((16, nx, ny), lambda i, off=off: (off + i, 0, 0)),
                pl.BlockSpec((16, nx, ny), lambda i: (i, 0, 0)),
                pl.BlockSpec((members, 16, nx, ny), lambda i, off=off: (0, off + i, 0, 0)),
                pl.BlockSpec((6, 16, ny), lambda i, off=off: (0, off + i, 0)),
            ],
            out_specs=pl.BlockSpec((16, 16, ny), lambda i: (i, 0, 0)),
            out_shape=jax.ShapeDtypeStruct((part, 16, ny), BF16),
            scratch_shapes=[pltpu.VMEM((16 * rows, ny), F32), pltpu.VMEM((16 * 16, ny), F32)],
            compiler_params=params(56),
            name=f"edges_{c}",
        )(g1, g2, ensemble, coef)
        if c == 0:
            h, *sides = lax.optimization_barrier((h, *sides))
            halo_u, halo_v = padded_winds(wind_u, wind_v, (before, after, *sides))
        h = lax.all_to_all(
            h.reshape(count_x, share, 16, ny), GX, split_axis=0, concat_axis=0, tiled=True
        )
        h = pl.pallas_call(
            scan_x_kernel,
            out_shape=jax.ShapeDtypeStruct(h.shape, BF16),
            in_specs=[vmem(), vmem()],
            out_specs=vmem(),
            compiler_params=params(8),
            name=f"scan_x_{c}",
        )(h, table_x)
        h = lax.all_to_all(h, GX, split_axis=0, concat_axis=0, tiled=True).reshape(part, 16, ny)
        hi, lo, es, to_right, to_left = pl.pallas_call(
            filter_x_kernel,
            grid=(steps,),
            in_specs=[
                pl.BlockSpec((16, nx, ny), lambda i, off=off: (off + i, 0, 0)),
                pl.BlockSpec((16, nx, ny), lambda i: (i, 0, 0)),
                pl.BlockSpec((members, 16, nx, ny), lambda i, off=off: (0, off + i, 0, 0)),
                pl.BlockSpec((16, 16, ny), lambda i: (i, 0, 0)),
                pl.BlockSpec((6, 16, ny), lambda i, off=off: (0, off + i, 0)),
                pl.BlockSpec((16, 16, ny), lambda i, off=off: (off + i, 0, 0)),
            ],
            out_specs=(
                pl.BlockSpec((16, deep, ny), lambda i: (i, 0, 0)),
                pl.BlockSpec((16, deep, ny), lambda i: (i, 0, 0)),
                pl.BlockSpec((count_y, 2, 16, deep), lambda i: (0, 0, i, 0)),
                pl.BlockSpec((3, 16, ny), lambda i: (0, i, 0)),
                pl.BlockSpec((3, 16, ny), lambda i: (0, i, 0)),
            ),
            out_shape=(
                jax.ShapeDtypeStruct((part, deep, ny), BF16),
                jax.ShapeDtypeStruct((part, deep, ny), BF16),
                jax.ShapeDtypeStruct((count_y, 2, part, deep), BF16),
                jax.ShapeDtypeStruct((3, part, ny), BF16),
                jax.ShapeDtypeStruct((3, part, ny), BF16),
            ),
            scratch_shapes=[
                pltpu.VMEM((16 * rows, ny), F32),
                pltpu.VMEM((16 * (deep + 8), ny), F32),
                pltpu.VMEM((16 * 16, ny), F32),
                pltpu.VMEM((16 * 16, ny), F32),
            ],
            compiler_params=params(56),
            name=f"filter_x_{c}",
        )(g1, g2, ensemble, h, coef, edge)
        es = lax.all_to_all(es, GY, split_axis=0, concat_axis=0, tiled=True)
        from_left = from_before(to_right, GY)
        from_right = from_after(to_left, GY)
        fb = pl.pallas_call(
            scan_y_kernel,
            out_shape=jax.ShapeDtypeStruct((part * 16, deep), BF16),
            in_specs=[smem()] + [vmem()] * 4,
            out_specs=vmem(),
            scratch_shapes=[
                pltpu.VMEM((count_y, part, deep), F32),
                pltpu.VMEM((count_y, part, deep), F32),
                pltpu.VMEM((2, part * 16, deep // 2), F32),
            ],
            compiler_params=params(16),
            name=f"scan_y_{c}",
        )(pos_y.reshape(1), es, from_left, from_right, coef_y[:, c * part : (c + 1) * part])
        steps = part // 8
        off = c * steps
        extra = () if c == 0 else (alpha, static)
        alpha, static = pl.pallas_call(
            final_kernel,
            grid=(steps,),
            in_specs=[
                pl.BlockSpec((8, deep, ny), lambda i: (i, 0, 0)),
                pl.BlockSpec((8, deep, ny), lambda i: (i, 0, 0)),
                pl.BlockSpec((8, ny, ny), lambda i, off=off: (off + i, 0, 0)),
                pl.BlockSpec((8, ny, ny), lambda i, off=off: (off + i, 0, 0)),
                pl.BlockSpec((8 * 16, deep), lambda i: (i, 0)),
                pl.BlockSpec((8, 16, 2 * ny), lambda i, off=off: (off + i, 0, 0)),
                pl.BlockSpec((8, nx + 8, 2 * ny), lambda i, off=off: (off + i, 0, 0)),
                pl.BlockSpec((8, nx + 8, 2 * ny), lambda i, off=off: (off + i, 0, 0)),
            ]
            + [pl.BlockSpec(memory_space=pl.ANY)] * len(extra),
            out_specs=(
                pl.BlockSpec((members, 8, nx, ny), lambda i, off=off: (0, off + i, 0, 0)),
                pl.BlockSpec((8, nx, ny), lambda i, off=off: (off + i, 0, 0)),
            ),
            out_shape=(
                jax.ShapeDtypeStruct((members, lev, nx, ny), F32),
                jax.ShapeDtypeStruct((lev, nx, ny), F32),
            ),
            input_output_aliases={8: 0, 9: 1} if extra else {},
            compiler_params=params(56),
            name=f"final_{c}",
        )(hi, lo, nh, nl, fb, spread, halo_u, halo_v, *extra)
    return alpha, static


def solution(mesh):
    grid = P(None, GX, GY)
    placed = (
        grid,
        P(None, None, GX, GY),
        grid,
        grid,
        P(),
        P(BOTH, None, None),
        P(BOTH, None),
        P(BOTH, None, None),
        P(BOTH),
        P(BOTH),
        P(BOTH),
    )
    return jax.shard_map(
        body,
        mesh=mesh,
        in_specs=placed,
        out_specs=(P(None, None, GX, GY), grid),
        check_vma=False,
    )
```
